32 devices in a mesh: dp: 16 (over z, y, x), mp: 2 (over core).
Axes of the slice: x: 2, y: 2, z: 4, core: 2. Of those that a mesh axis runs over, the one named last changes fastest.
Arguments:
- tokens: bfloat16 [8192, 2048], P('dp'), may hold values from -6 to 6
- q_weight: bfloat16 [2048, 256], P('dp', 'mp'), may hold values from -0.125 to 0.125
- k_weight: bfloat16 [2048, 256], P('dp', 'mp'), may hold values from -0.125 to 0.125
- v_weight: bfloat16 [2048, 2048], P('dp', 'mp'), may hold values from -0.125 to 0.125
- adapter_down: bfloat16 [2048, 256], P(None, 'mp'), may hold values from -0.125 to 0.125
- adapter_up: bfloat16 [256, 2048], P(None, 'mp'), may hold values from -1.5 to 1.5
- lengths: int32 [4], replicated, may hold values from 1 to 4096, 8192 in all
- adapter_ids: int32 [4], replicated, may hold values from 0 to 15
- head_gain: float32 [2048], P('mp'), may hold values from 0.1 to 1.9
- out_weight: bfloat16 [2048, 2048], P('mp', 'dp'), may hold values from -0.125 to 0.125
Outputs:
- layer_out: bfloat16 [8192, 2048], P('dp', 'mp')
The draws below stay inside these ranges and needn't reach their ends.
Inputs may be any that keep to these rules, and one draw needn't show every extreme that they name: The lengths sum to 8192 and the longest request has exactly 8192 // 2 tokens.
All inputs are finite; a program needn't handle non-finite values.
Results may differ from the reference program's by a relative error of at most 0.022.
Values may be sent and summed in bfloat16 or wider, within the bound.
No kernel may reach another device: no remote copies, remote signals or barrier semaphores. Data moves between devices by JAX's collectives and lax.ppermute only.
A program may use at most 128 MiB of HBM per device.

```python
import math
import jax
import jax.numpy as jnp
import numpy as np
from jax import lax

D = 2048
H = 16
F = 16
R = 16
ADAPTERS = 16
REQS = 4
TOK_DEV = 512
DV = 128
FEATS = 273
TOKENS = 8192


def place_ends(drawn, rng, smallest, high):
    shape = drawn.shape
    index_at = [jax.random.randint(jax.random.fold_in(rng, axis), (), 0, shape[axis]) for axis in range(len(shape))]
    drawn = drawn.at[tuple(index_at)].set(smallest)
    longest = shape.index(max(shape))
    index_at[longest] = (index_at[longest] + 1) % shape[longest]
    return drawn.at[tuple(index_at)].set(high)


def levels(key, dims, shards, low, high):
    factor_of, own = 1.0, jax.random.fold_in(key, 6)
    for axis_at, parts in shards:
        steps = jnp.exp(jax.random.uniform(jax.random.fold_in(own, axis_at), (parts,), jnp.float32, low / len(shards), high / len(shards)))
        factor_of = factor_of * jnp.repeat(steps, dims[axis_at] // parts).reshape([-1 if axis == axis_at else 1 for axis in range(len(dims))])
    return factor_of


def split_up(count, total, most, slope):
    loads = [(1 << 20) // math.isqrt(grade ** slope) + 1 for grade in range(2, count + 1)]
    spare, holding = total - most - (count - 1), [1] * (count - 1)
    while spare > 0:
        movable = [i for i in range(count - 1) if holding[i] < most]
        mass, remaining = sum([loads[i] for i in movable]), spare
        for i in movable:
            addition = min(most - holding[i], max(1, remaining * loads[i] // mass), spare)
            holding[i] = holding[i] + addition
            spare = spare - addition
    return np.array([most] + holding)


def ragged(key, number_of, total, reach, skew):
    if number_of == 2:
        one = jax.random.randint(key, (), max(1, total - reach), min(reach, total - 1) + 1)
        return jnp.stack([one, total - one])
    sizes = jnp.asarray(split_up(number_of, total, reach, skew), jnp.int32)
    couples = (number_of - 1) // 2
    giver, receiver = sizes[1:1 + 2 * couples:2], sizes[2:2 + 2 * couples:2]
    margin = jnp.minimum(giver - 1, reach - receiver)
    moved = jax.random.randint(jax.random.fold_in(key, 1), (couples,), 0, 1 << 20) % (margin + 1)
    sizes = sizes.at[1:1 + 2 * couples:2].set(giver - moved).at[2:2 + 2 * couples:2].set(receiver + moved)
    return sizes[jax.random.permutation(jax.random.fold_in(key, 2), number_of)]


def noise(own_key, dims, scale, limit, split=(), held_as=jnp.bfloat16):
    level = levels(own_key, dims, split, -0.22, 0.18) if split else 1.0
    values = jax.random.normal(own_key, dims, jnp.float32) * scale * level
    return jnp.minimum(jnp.maximum(values, -limit), limit).astype(held_as)


def setup_inputs(seed: int = 0) -> dict:
    key_list = jax.random.split(jax.random.key(seed), 11)
    tokens = noise(key_list[0], (TOKENS, D), 1.0, 6.0, ((0, 16),))
    q_weight = noise(key_list[1], (D, H * F), D ** -0.5, 0.125, ((0, 16), (1, 2)))
    k_weight = noise(key_list[2], (D, H * F), D ** -0.5, 0.125, ((0, 16), (1, 2)))
    v_weight = noise(key_list[3], (D, D), D ** -0.5, 0.125, ((0, 16), (1, 2)))
    adapter_down = noise(key_list[4], (D, ADAPTERS * R), D ** -0.5, 0.125, ((1, 2),))
    adapter_up = noise(key_list[5], (ADAPTERS * R, D), R ** -0.5, 1.5, ((1, 2),))
    lengths = ragged(key_list[6], REQS, TOKENS, TOKENS // 2, 2).astype(jnp.int32)
    adapter_ids = place_ends(jax.random.randint(key_list[7], (REQS,), 0, ADAPTERS), jax.random.fold_in(key_list[7], 1), 0, ADAPTERS - 1).astype(jnp.int32)
    head_gain = jnp.clip(1.0 + 0.18 * jax.random.normal(key_list[8], (D,), jnp.float32), 0.1, 1.9)
    out_weight = noise(key_list[9], (D, D), D ** -0.5, 0.125, ((0, 2), (1, 16)))
    return {"tokens": tokens, "q_weight": q_weight, "k_weight": k_weight, "v_weight": v_weight, "adapter_down": adapter_down, "adapter_up": adapter_up, "lengths": lengths, "adapter_ids": adapter_ids, "head_gain": head_gain, "out_weight": out_weight}


EPSILON = 1e-05

def taylor(inputs):
    squares = (inputs[..., :, None] * inputs[..., None, :]).reshape(inputs.shape[:-1] + (inputs.shape[-1] * inputs.shape[-1],))
    constant = jnp.ones(inputs.shape[:-1] + (1,), jnp.float32)
    return jnp.concatenate([constant, 0.5 * inputs, squares * (0.25 / math.sqrt(2.0))], axis=-1)

def token_tables(lengths, adapter_ids, positions):
    bounds = jnp.cumsum(lengths).astype(jnp.int32)
    request = lax.optimization_barrier(jnp.sum((positions[:, None] >= bounds[None, :]).astype(jnp.int32), axis=1)).astype(jnp.int32)
    openings = (bounds - lengths).astype(jnp.int32)
    starts = jnp.any(positions[:, None] == openings[None, :], axis=1)
    picked = request[:, None] == jnp.arange(lengths.shape[0], dtype=jnp.int32)[None, :]
    adapter = lax.optimization_barrier(jnp.sum(jnp.where(picked, adapter_ids[None, :], 0), axis=1)).astype(jnp.int32)
    return (request, starts, adapter)

def block_local(query, key_rows, values, request, starts):
    scores = jnp.einsum('ihd,jhd->hij', query.astype(jnp.float32), key_rows.astype(jnp.float32)) * 0.25
    weights = 1.0 + scores + 0.5 * scores * scores
    indexes = jnp.arange(request.shape[0], dtype=jnp.int32)
    allowed = (indexes[None, :] <= indexes[:, None]) & (request[None, :] == request[:, None])
    weights = jnp.where(allowed[None], weights, 0.0).astype(jnp.bfloat16)
    within = jnp.einsum('hij,jhe->ihe', weights.astype(jnp.float32), values.astype(jnp.float32))
    query_map = taylor(query.astype(jnp.float32)).astype(jnp.bfloat16)
    key_map = taylor(key_rows.astype(jnp.float32)).astype(jnp.bfloat16)
    tail_mask = (request == request[-1]).astype(jnp.bfloat16)
    masked_keys = key_map * tail_mask[:, None, None]
    summary = jnp.einsum('ihf,ihe->hfe', masked_keys.astype(jnp.float32), values.astype(jnp.float32))
    restart = jnp.max(starts.astype(jnp.float32))
    return (within, query_map, summary, restart)

def finish(within, query_map, carried, request, starts, gains):
    follows = ((request == request[0]) & jnp.logical_not(starts[0])).astype(jnp.float32)
    cross = jnp.einsum('ihf,hfe->ihe', query_map.astype(jnp.float32), carried.astype(jnp.bfloat16).astype(jnp.float32))
    combined = within + follows[:, None, None] * cross
    factor = lax.rsqrt(lax.optimization_barrier(jnp.mean(combined * combined, axis=-1, keepdims=True)) + EPSILON)
    return (combined * factor * gains[None]).astype(jnp.bfloat16)

def reference(tokens, q_weight, k_weight, v_weight, adapter_down, adapter_up, lengths, adapter_ids, head_gain, out_weight):
    total_rows = tokens.shape[0]
    positions = jnp.arange(total_rows, dtype=jnp.int32)
    request, starts, adapter = token_tables(lengths, adapter_ids, positions)
    query = jnp.dot(tokens, q_weight, preferred_element_type=jnp.float32).astype(jnp.bfloat16).reshape(total_rows, H, F)
    key_rows = jnp.dot(tokens, k_weight, preferred_element_type=jnp.float32).astype(jnp.bfloat16).reshape(total_rows, H, F)
    low_rank = jnp.dot(tokens, adapter_down, preferred_element_type=jnp.float32)
    owners = jnp.arange(ADAPTERS * R, dtype=jnp.int32) // R
    low_rank = jnp.where(adapter[:, None] == owners[None, :], low_rank, 0.0).astype(jnp.bfloat16)
    values = jnp.dot(tokens, v_weight, preferred_element_type=jnp.float32) + jnp.dot(low_rank, adapter_up, preferred_element_type=jnp.float32)
    values = values.astype(jnp.bfloat16).reshape(total_rows, H, DV)
    gains = head_gain.reshape(H, DV)
    block_count = total_rows // TOK_DEV

    def by_block(array):
        return array.reshape((block_count, TOK_DEV) + array.shape[1:])

    def advance(carried, pieces):
        block_query, block_keys, block_values, block_request, block_starts = pieces
        within, query_map, summary, restart = block_local(block_query, block_keys, block_values, block_request, block_starts)
        normed = finish(within, query_map, carried, block_request, block_starts, gains)
        following = jnp.where(restart > 0, summary, carried + summary)
        return (following, normed)
    initial = jnp.zeros((H, FEATS, DV), jnp.float32)
    _, normed = lax.scan(advance, initial, (by_block(query), by_block(key_rows), by_block(values), by_block(request), by_block(starts)))
    normed = normed.reshape(total_rows, D)
    return jnp.dot(normed, out_weight, preferred_element_type=jnp.float32).astype(jnp.bfloat16)
```

```python
import functools
import math

import jax
import jax.numpy as jnp
import numpy as np
from jax import lax
from jax.experimental import pallas as pl
from jax.experimental.pallas import tpu as pltpu
from jax.sharding import PartitionSpec as P

F = 16
R = 16
EPSILON = 1e-05
SQUARES = [(a, b) for a in range(F) for b in range(a, F)]
FEATS = 160
VMEM_LIMIT = 56 * 1024 * 1024
VMEM = pl.BlockSpec(memory_space=pltpu.VMEM)
SMEM = pl.BlockSpec(memory_space=pltpu.SMEM)


def carried_in(value, axis, combine, identity):
    length, place = (lax.axis_size(axis), lax.axis_index(axis))
    everything = jax.tree.map(
        lambda part, kind: lax.all_gather(part.astype(kind), axis),
        value,
        (jnp.bfloat16, jnp.bfloat16),
    )
    start = jax.tree.map(
        lambda part, zero: jnp.broadcast_to(jnp.asarray(zero, part.dtype), part.shape),
        value,
        identity,
    )

    def turn(k, before):
        reached = k < place
        new = combine(
            before, jax.tree.map(lambda part, own: part[k].astype(own.dtype), everything, value)
        )
        return jax.tree.map(lambda a, b: jnp.where(reached, a, b), new, before)

    return lax.fori_loop(0, length, turn, start)


def taylor(inputs):
    squares = (inputs[..., :, None] * inputs[..., None, :]).reshape(
        inputs.shape[:-1] + (inputs.shape[-1] * inputs.shape[-1],)
    )
    constant = jnp.ones(inputs.shape[:-1] + (1,), jnp.float32)
    return jnp.concatenate([constant, 0.5 * inputs, squares * (0.25 / math.sqrt(2.0))], axis=-1)


def token_tables(lengths, adapter_ids, positions):
    bounds = jnp.cumsum(lengths)
    request = jnp.sum((positions[:, None] >= bounds[None, :]).astype(jnp.int32), axis=1)
    openings = bounds - lengths
    starts = jnp.any(positions[:, None] == openings[None, :], axis=1)
    picked = request[:, None] == jnp.arange(lengths.shape[0], dtype=jnp.int32)[None, :]
    adapter = jnp.sum(jnp.where(picked, adapter_ids[None, :], 0), axis=1)
    return (request, starts, adapter)


def block_local(query, key_rows, values, request, starts):
    scores = jnp.einsum("ihd,jhd->hij", query, key_rows, preferred_element_type=jnp.float32) * 0.25
    weights = 1.0 + scores + 0.5 * scores * scores
    indexes = jnp.arange(request.shape[0], dtype=jnp.int32)
    allowed = (indexes[None, :] <= indexes[:, None]) & (request[None, :] == request[:, None])
    weights = jnp.where(allowed[None], weights, 0.0).astype(jnp.bfloat16)
    within = jnp.einsum("hij,jhe->ihe", weights, values, preferred_element_type=jnp.float32)
    query_map = taylor(query.astype(jnp.float32)).astype(jnp.bfloat16)
    key_map = taylor(key_rows.astype(jnp.float32)).astype(jnp.bfloat16)
    tail_mask = (request == request[-1]).astype(jnp.bfloat16)
    masked_keys = key_map * tail_mask[:, None, None]
    summary = jnp.einsum("ihf,ihe->hfe", masked_keys, values, preferred_element_type=jnp.float32)
    restart = jnp.max(starts.astype(jnp.float32))
    return (within, query_map, summary, restart)


def finish(within, query_map, carried, request, starts, gains):
    follows = ((request == request[0]) & jnp.logical_not(starts[0])).astype(jnp.float32)
    cross = jnp.einsum(
        "ihf,hfe->ihe", query_map, carried.astype(jnp.bfloat16), preferred_element_type=jnp.float32
    )
    combined = within + follows[:, None, None] * cross
    factor = lax.rsqrt(jnp.mean(combined * combined, axis=-1, keepdims=True) + EPSILON)
    return (combined * factor * gains[None]).astype(jnp.bfloat16)


def combine(earlier, later):
    return (
        jnp.maximum(earlier[0], later[0]),
        jnp.where(later[0] > 0, later[1], earlier[1] + later[1]),
    )


def per_device_general(
    tokens,
    q_weight,
    k_weight,
    v_weight,
    adapter_down,
    adapter_up,
    lengths,
    adapter_ids,
    head_gain,
    out_weight,
):
    row_count = tokens.shape[0]
    heads_here = q_weight.shape[1] // F
    value_width = v_weight.shape[1] // heads_here
    positions = lax.axis_index("dp") * row_count + jnp.arange(row_count, dtype=jnp.int32)
    request, starts, adapter = token_tables(lengths, adapter_ids, positions)
    together = lax.all_gather(
        jnp.concatenate([q_weight, k_weight, v_weight], axis=1), "dp", axis=0, tiled=True
    )
    sums = jnp.dot(tokens, together, preferred_element_type=jnp.float32)
    width = heads_here * F
    query = sums[:, :width].astype(jnp.bfloat16).reshape(row_count, heads_here, F)
    key_rows = sums[:, width : 2 * width].astype(jnp.bfloat16).reshape(row_count, heads_here, F)
    value_sum = sums[:, 2 * width :]
    piece = lax.all_gather(adapter_down, "mp", axis=1, tiled=True)
    partial_low = jnp.dot(tokens, piece, preferred_element_type=jnp.float32)
    owners = jnp.arange(piece.shape[1], dtype=jnp.int32) // R
    low_rank = jnp.where(adapter[:, None] == owners[None, :], partial_low, 0.0).astype(jnp.bfloat16)
    values = value_sum + jnp.dot(low_rank, adapter_up, preferred_element_type=jnp.float32)
    values = values.astype(jnp.bfloat16).reshape(row_count, heads_here, value_width)
    within, query_map, summary, restart = block_local(query, key_rows, values, request, starts)
    identity = (jnp.zeros((), jnp.float32), jnp.zeros_like(summary))
    _, carried = carried_in((restart, summary), "dp", combine, identity)
    gains = head_gain.reshape(heads_here, value_width)
    normed = finish(within, query_map, carried, request, starts, gains).reshape(
        row_count, heads_here * value_width
    )
    partial_terms = jnp.dot(
        normed,
        lax.all_gather(out_weight, "dp", axis=1, tiled=True),
        preferred_element_type=jnp.float32,
    )
    return lax.psum_scatter(
        partial_terms.astype(jnp.bfloat16), "mp", scatter_dimension=1, tiled=True
    )


def feature_tables(heads):
    first = np.zeros((heads, FEATS, heads * F), np.float32)
    second = np.zeros((heads, FEATS, heads * F), np.float32)
    scale = np.zeros((8, FEATS), np.float32)
    scale[0, 0] = scale[1, 0] = scale[2, 0] = scale[3, 0] = 1.0
    for a in range(F):
        first[np.arange(heads), 1 + a, np.arange(heads) * F + a] = 1.0
        scale[1, 1 + a] = 1.0
        scale[2, 1 + a] = scale[3, 1 + a] = 0.5
    for at, (a, b) in enumerate(SQUARES):
        row = 1 + F + at
        first[np.arange(heads), row, np.arange(heads) * F + a] = 1.0
        second[np.arange(heads), row, np.arange(heads) * F + b] = 1.0
        scale[2, row] = 0.25 / math.sqrt(2.0)
        scale[3, row] = (0.25 if a == b else 0.5) / math.sqrt(2.0)
    return first.astype(jnp.bfloat16), second.astype(jnp.bfloat16), scale


def chip(place, x):
    z, y = (place, 0) if place < 4 else (7 - place, 1)
    return z * 4 + y * 2 + x


def moves(step, flip):
    return [
        (chip(r, x), chip((r + step) % 8, x ^ flip)) for r in range(8) for x in range(2)
    ]


UP, DOWN, ACROSS = moves(1, 0), moves(-1, 0), moves(0, 1)


def ring_places():
    here = lax.axis_index("dp")
    z, y, x = here // 4, (here // 2) % 2, here % 2
    place = jnp.where(y == 0, z, 7 - z)
    there = (place + jnp.arange(8, dtype=jnp.int32)) % 8
    base = jnp.where(there < 4, there * 4, (7 - there) * 4 + 2)
    return jnp.concatenate([base + x, base + 1 - x]).astype(jnp.int32)


def send(value, pairs):
    return lax.ppermute(value, "dp", pairs)


def gather_rows(block):
    rows = block.shape[0]
    half, quarter = rows // 2, rows // 4
    alone, pair = block[:half], block[half:]
    pair = jnp.concatenate([pair, send(pair, ACROSS)], axis=0)

    def ring(piece):
        middle = piece.shape[0] // 2
        up, down = [piece], [piece]
        for _ in range(3):
            up.append(send(up[-1], UP))
            down.append(send(down[-1], DOWN))
        up.append(send(up[-1][:middle], UP))
        down.append(send(down[-1][middle:], DOWN))
        return up, down

    pieces = []
    up, down = ring(alone)
    for k in range(4):
        for distance, piece in ((-k % 8, up[k]), (k, down[k]))[: 1 if k == 0 else 2]:
            pieces.append((piece, [(distance, 0, half, 0)]))
            pieces.append((send(piece, ACROSS), [(8 + distance, 0, half, 0)]))
    for piece, row in ((up[4], 0), (down[4], quarter)):
        pieces.append((piece, [(4, row, quarter, 0)]))
        pieces.append((send(piece, ACROSS), [(12, row, quarter, 0)]))
    up, down = ring(pair)
    for k in range(4):
        for distance, piece in ((-k % 8, up[k]), (k, down[k]))[: 1 if k == 0 else 2]:
            pieces.append(
                (piece, [(distance, half, half, 0), (8 + distance, half, half, half)])
            )
    pieces.append((up[4], [(4, half, half, 0)]))
    pieces.append((down[4], [(12, half, half, 0)]))
    return pieces


NT = (((1,), (1,)), ((), ()))


def project_kernel(layout, rows, heads, width, slots, tokens, low, up, tail, first, second, scale,
                   *refs):
    pieces, (query, keys, values, state, held) = refs[: len(layout)], refs[len(layout) :]
    for piece, places in zip(pieces, layout):
        for slot, row, count, source in places:
            at = pl.multiple_of(slots[slot] * rows + row, rows // 4)
            held[pl.ds(at, count), :] = piece[source : source + count, :]
    wide = heads * width
    small = heads * F
    both = jnp.dot(tokens[...], held[:, wide:], preferred_element_type=jnp.float32)
    query[...] = both[:, :small].astype(jnp.bfloat16)
    key_rows = both[:, small:].astype(jnp.bfloat16)
    keys[...] = key_rows
    for h in range(0, heads, 2):
        cols = slice(h * width, (h + 2) * width)
        total = jnp.dot(tokens[...], held[:, cols], preferred_element_type=jnp.float32)
        total += jnp.dot(low[...], up[:, cols], preferred_element_type=jnp.float32)
        values[:, cols] = total.astype(jnp.bfloat16)
        for g in (h, h + 1):
            a = lax.dot_general(first[g], key_rows, NT, preferred_element_type=jnp.float32)
            b = lax.dot_general(second[g], key_rows, NT, preferred_element_type=jnp.float32)
            mapped = ((a + scale[:, 0:1]) * (b + scale[:, 1:2])) * scale[:, 2:3]
            mapped = (mapped * tail[...]).astype(jnp.bfloat16)
            state[g] = jnp.dot(
                mapped, values[:, g * width : (g + 1) * width], preferred_element_type=jnp.float32
            ).astype(jnp.bfloat16)


def within_kernel(heads, width, query, keys, values, row, col, within):
    count = query.shape[0]
    cut = count // 2
    lanes = lax.broadcasted_iota(jnp.int32, (1, heads * F), 1)
    parts = ((0, cut), (cut, count))
    for low, high in parts:
        i = lax.broadcasted_iota(jnp.int32, (high - low, high), 0) + low
        j = lax.broadcasted_iota(jnp.int32, (high - low, high), 1)
        allowed = (j <= i) & (row[:, :high] == col[low:high, :])
        for h in range(heads):
            mine = jnp.where(lanes // F == h, 0.25, 0.0).astype(jnp.bfloat16)
            s = lax.dot_general(
                query[low:high, :] * mine, keys[:high, :], NT, preferred_element_type=jnp.float32
            )
            weights = 1.0 + s + 0.5 * s * s
            weights = jnp.where(allowed, weights, 0.0).astype(jnp.bfloat16)
            cols = slice(h * width, (h + 1) * width)
            within[low:high, cols] = jnp.dot(
                weights, values[:high, cols], preferred_element_type=jnp.float32
            )


def mix_kernel(blocks, marks, states, mixed):
    for b in range(blocks):
        total = jnp.zeros(states.shape[1:], jnp.float32)
        for e in range(b):
            total += marks[b * blocks + e] * states[e].astype(jnp.float32)
        mixed[b] = total.astype(jnp.bfloat16)


def finish_kernel(heads, width, within, query, carried, first, second, scale, follows, gains,
                  normed):
    rows = query[...]
    for h in range(heads):
        a = lax.dot_general(rows, first[h], NT, preferred_element_type=jnp.float32)
        b = lax.dot_general(rows, second[h], NT, preferred_element_type=jnp.float32)
        mapped = ((a + scale[0:1, :]) * (b + scale[1:2, :])) * scale[3:4, :]
        cross = jnp.dot(mapped.astype(jnp.bfloat16), carried[h], preferred_element_type=jnp.float32)
        cols = slice(h * width, (h + 1) * width)
        combined = within[:, cols] + follows[...] * cross
        factor = lax.rsqrt(jnp.mean(combined * combined, axis=-1, keepdims=True) + EPSILON)
        normed[:, cols] = (combined * factor * gains[:, cols]).astype(jnp.bfloat16)


def out_kernel(which, normed, weight, out):
    out[...] = jnp.dot(normed[...], weight[...], preferred_element_type=jnp.float32).astype(
        out.dtype
    )


def out_half(which, normed, weight, kind):
    rows, depth = normed.shape
    half = weight.shape[1] // 2
    tile = 256
    return pl.pallas_call(
        out_kernel,
        out_shape=jax.ShapeDtypeStruct((rows, half), kind),
        grid_spec=pltpu.PrefetchScalarGridSpec(
            num_scalar_prefetch=1,
            grid=(half // tile,),
            in_specs=[
                pl.BlockSpec((rows, depth), lambda j, s: (0, 0)),
                pl.BlockSpec((depth, tile), lambda j, s: (0, s[0] * (half // tile) + j)),
            ],
            out_specs=pl.BlockSpec((rows, tile), lambda j, s: (0, j)),
        ),
        compiler_params=pltpu.CompilerParams(vmem_limit_bytes=VMEM_LIMIT),
        cost_estimate=pl.CostEstimate(
            flops=2 * rows * depth * half, bytes_accessed=2 * depth * half, transcendentals=0
        ),
        name="out_half",
    )(which, normed, weight)


def per_device_fast(
    tokens,
    q_weight,
    k_weight,
    v_weight,
    adapter_down,
    adapter_up,
    lengths,
    adapter_ids,
    head_gain,
    out_weight,
):
    count, depth = tokens.shape
    blocks = lax.axis_size("dp")
    heads = q_weight.shape[1] // F
    width = v_weight.shape[1] // heads
    here, core = lax.axis_index("dp"), lax.axis_index("mp")
    params = pltpu.CompilerParams(vmem_limit_bytes=VMEM_LIMIT)

    out_all = lax.all_gather(out_weight, "dp", axis=1, tiled=True)

    positions = here * count + jnp.arange(count, dtype=jnp.int32)
    request, starts, adapter = token_tables(lengths, adapter_ids, positions)
    bounds = jnp.cumsum(lengths)
    opens = jnp.arange(blocks, dtype=jnp.int32) * count
    ends = opens + (count - 1)
    first_request = jnp.sum((opens[:, None] >= bounds[None, :]).astype(jnp.int32), axis=1)
    last_request = jnp.sum((ends[:, None] >= bounds[None, :]).astype(jnp.int32), axis=1)
    marks = (first_request[:, None] == last_request[None, :]).astype(jnp.float32).reshape(-1)
    tail = (request == request[-1]).astype(jnp.float32).reshape(1, count)
    follows = (request == request[0]).astype(jnp.float32).reshape(count, 1)

    other = lax.ppermute(adapter_down, "mp", [(0, 1), (1, 0)])
    wide = adapter_down.shape[1]
    owners = jnp.arange(wide, dtype=jnp.int32) // R
    lows = []
    for piece, place in ((adapter_down, core), (other, 1 - core)):
        partial = jnp.dot(tokens, piece, preferred_element_type=jnp.float32)
        kept = adapter[:, None] == owners[None, :] + place * (wide // R)
        lows.append(jnp.where(kept, partial, 0.0).astype(jnp.bfloat16))
    low = jnp.where(core == 0, jnp.concatenate(lows, 1), jnp.concatenate(lows[::-1], 1))

    first, second, scale = feature_tables(heads)
    first, second, scale = jnp.asarray(first), jnp.asarray(second), jnp.asarray(scale)

    rows = v_weight.shape[0]
    gathered = gather_rows(jnp.concatenate([v_weight, q_weight, k_weight], axis=1))
    layout = [places for _, places in gathered]
    pieces = [piece for piece, _ in gathered]
    total_width = heads * (width + 2 * F)
    query, keys, values, state = pl.pallas_call(
        functools.partial(project_kernel, layout, rows, heads, width),
        out_shape=(
            jax.ShapeDtypeStruct((count, heads * F), jnp.bfloat16),
            jax.ShapeDtypeStruct((count, heads * F), jnp.bfloat16),
            jax.ShapeDtypeStruct((count, heads * width), jnp.bfloat16),
            jax.ShapeDtypeStruct((heads, FEATS, width), jnp.bfloat16),
        ),
        in_specs=[SMEM] + [VMEM] * (7 + len(pieces)),
        out_specs=(VMEM,) * 4,
        scratch_shapes=[pltpu.VMEM((depth, total_width), jnp.bfloat16)],
        compiler_params=params,
        cost_estimate=pl.CostEstimate(
            flops=2 * count * depth * total_width, bytes_accessed=2 * depth * total_width * 2,
            transcendentals=0,
        ),
        name="project",
    )(ring_places(), tokens, low, adapter_up, tail, first, second, scale.T, *pieces)

    parts = state.reshape(blocks, heads * FEATS // blocks, width)
    parts = lax.all_to_all(parts, "dp", 0, 0, tiled=True)
    mixed = pl.pallas_call(
        functools.partial(mix_kernel, blocks),
        out_shape=jax.ShapeDtypeStruct(parts.shape, jnp.bfloat16),
        in_specs=[SMEM, VMEM],
        out_specs=VMEM,
        compiler_params=params,
        name="mix",
    )(marks, parts)
    carried = lax.all_to_all(mixed, "dp", 0, 0, tiled=True).reshape(heads, FEATS, width)

    within = pl.pallas_call(
        functools.partial(within_kernel, heads, width),
        out_shape=jax.ShapeDtypeStruct((count, heads * width), jnp.float32),
        in_specs=[VMEM] * 5,
        out_specs=VMEM,
        compiler_params=params,
        cost_estimate=pl.CostEstimate(
            flops=4 * count * count * width * heads, bytes_accessed=4 * count * heads * width,
            transcendentals=0,
        ),
        name="within",
    )(query, keys, values, request.reshape(1, count), request.reshape(count, 1))

    normed = pl.pallas_call(
        functools.partial(finish_kernel, heads, width),
        out_shape=jax.ShapeDtypeStruct((count, heads * width), jnp.bfloat16),
        in_specs=[VMEM] * 8,
        out_specs=VMEM,
        compiler_params=params,
        cost_estimate=pl.CostEstimate(
            flops=4 * count * FEATS * width * heads, bytes_accessed=4 * count * heads * width,
            transcendentals=0,
        ),
        name="finish",
    )(within, query, carried, first, second, scale, follows, head_gain.reshape(1, -1))

    theirs = out_half((1 - core).reshape(1).astype(jnp.int32), normed, out_all, jnp.bfloat16)
    received = lax.ppermute(theirs, "mp", [(0, 1), (1, 0)])
    mine = out_half(core.reshape(1).astype(jnp.int32), normed, out_all, jnp.float32)
    return (mine + received.astype(jnp.float32)).astype(jnp.bfloat16)


def solution(mesh):
    placed = (
        P("dp", None),
        P("dp", "mp"),
        P("dp", "mp"),
        P("dp", "mp"),
        P(None, "mp"),
        P(None, "mp"),
        P(),
        P(),
        P("mp"),
        P("mp", "dp"),
    )
    fast = mesh.shape["dp"] == 16 and mesh.shape["mp"] == 2
    return jax.shard_map(
        per_device_fast if fast else per_device_general,
        mesh=mesh,
        in_specs=placed,
        out_specs=P("dp", "mp"),
        check_vma=False,
    )
```

```python
import functools
import math

import jax
import jax.numpy as jnp
import numpy as np
from jax import lax
from jax.experimental import pallas as pl
from jax.experimental.pallas import tpu as pltpu
from jax.sharding import PartitionSpec as P

F = 16
R = 16
EPSILON = 1e-05
SQUARES = [(a, b) for a in range(F) for b in range(a, F)]
FEATS = 160
VMEM_LIMIT = 56 * 1024 * 1024
VMEM = pl.BlockSpec(memory_space=pltpu.VMEM)
SMEM = pl.BlockSpec(memory_space=pltpu.SMEM)
ANY = pl.BlockSpec(memory_space=pl.ANY)


def carried_in(value, axis, combine, identity):
    length, place = (lax.axis_size(axis), lax.axis_index(axis))
    everything = jax.tree.map(
        lambda part, kind: lax.all_gather(part.astype(kind), axis),
        value,
        (jnp.bfloat16, jnp.bfloat16),
    )
    start = jax.tree.map(
        lambda part, zero: jnp.broadcast_to(jnp.asarray(zero, part.dtype), part.shape),
        value,
        identity,
    )

    def turn(k, before):
        reached = k < place
        new = combine(
            before, jax.tree.map(lambda part, own: part[k].astype(own.dtype), everything, value)
        )
        return jax.tree.map(lambda a, b: jnp.where(reached, a, b), new, before)

    return lax.fori_loop(0, length, turn, start)


def taylor(inputs):
    squares = (inputs[..., :, None] * inputs[..., None, :]).reshape(
        inputs.shape[:-1] + (inputs.shape[-1] * inputs.shape[-1],)
    )
    constant = jnp.ones(inputs.shape[:-1] + (1,), jnp.float32)
    return jnp.concatenate([constant, 0.5 * inputs, squares * (0.25 / math.sqrt(2.0))], axis=-1)


def token_tables(lengths, adapter_ids, positions):
    bounds = jnp.cumsum(lengths)
    request = jnp.sum((positions[:, None] >= bounds[None, :]).astype(jnp.int32), axis=1)
    openings = bounds - lengths
    starts = jnp.any(positions[:, None] == openings[None, :], axis=1)
    picked = request[:, None] == jnp.arange(lengths.shape[0], dtype=jnp.int32)[None, :]
    adapter = jnp.sum(jnp.where(picked, adapter_ids[None, :], 0), axis=1)
    return (request, starts, adapter)


def block_local(query, key_rows, values, request, starts):
    scores = jnp.einsum("ihd,jhd->hij", query, key_rows, preferred_element_type=jnp.float32) * 0.25
    weights = 1.0 + scores + 0.5 * scores * scores
    indexes = jnp.arange(request.shape[0], dtype=jnp.int32)
    allowed = (indexes[None, :] <= indexes[:, None]) & (request[None, :] == request[:, None])
    weights = jnp.where(allowed[None], weights, 0.0).astype(jnp.bfloat16)
    within = jnp.einsum("hij,jhe->ihe", weights, values, preferred_element_type=jnp.float32)
    query_map = taylor(query.astype(jnp.float32)).astype(jnp.bfloat16)
    key_map = taylor(key_rows.astype(jnp.float32)).astype(jnp.bfloat16)
    tail_mask = (request == request[-1]).astype(jnp.bfloat16)
    masked_keys = key_map * tail_mask[:, None, None]
    summary = jnp.einsum("ihf,ihe->hfe", masked_keys, values, preferred_element_type=jnp.float32)
    restart = jnp.max(starts.astype(jnp.float32))
    return (within, query_map, summary, restart)


def finish(within, query_map, carried, request, starts, gains):
    follows = ((request == request[0]) & jnp.logical_not(starts[0])).astype(jnp.float32)
    cross = jnp.einsum(
        "ihf,hfe->ihe", query_map, carried.astype(jnp.bfloat16), preferred_element_type=jnp.float32
    )
    combined = within + follows[:, None, None] * cross
    factor = lax.rsqrt(jnp.mean(combined * combined, axis=-1, keepdims=True) + EPSILON)
    return (combined * factor * gains[None]).astype(jnp.bfloat16)


def combine(earlier, later):
    return (
        jnp.maximum(earlier[0], later[0]),
        jnp.where(later[0] > 0, later[1], earlier[1] + later[1]),
    )


def per_device_general(
    tokens,
    q_weight,
    k_weight,
    v_weight,
    adapter_down,
    adapter_up,
    lengths,
    adapter_ids,
    head_gain,
    out_weight,
):
    row_count = tokens.shape[0]
    heads_here = q_weight.shape[1] // F
    value_width = v_weight.shape[1] // heads_here
    positions = lax.axis_index("dp") * row_count + jnp.arange(row_count, dtype=jnp.int32)
    request, starts, adapter = token_tables(lengths, adapter_ids, positions)
    together = lax.all_gather(
        jnp.concatenate([q_weight, k_weight, v_weight], axis=1), "dp", axis=0, tiled=True
    )
    sums = jnp.dot(tokens, together, preferred_element_type=jnp.float32)
    width = heads_here * F
    query = sums[:, :width].astype(jnp.bfloat16).reshape(row_count, heads_here, F)
    key_rows = sums[:, width : 2 * width].astype(jnp.bfloat16).reshape(row_count, heads_here, F)
    value_sum = sums[:, 2 * width :]
    piece = lax.all_gather(adapter_down, "mp", axis=1, tiled=True)
    partial_low = jnp.dot(tokens, piece, preferred_element_type=jnp.float32)
    owners = jnp.arange(piece.shape[1], dtype=jnp.int32) // R
    low_rank = jnp.where(adapter[:, None] == owners[None, :], partial_low, 0.0).astype(jnp.bfloat16)
    values = value_sum + jnp.dot(low_rank, adapter_up, preferred_element_type=jnp.float32)
    values = values.astype(jnp.bfloat16).reshape(row_count, heads_here, value_width)
    within, query_map, summary, restart = block_local(query, key_rows, values, request, starts)
    identity = (jnp.zeros((), jnp.float32), jnp.zeros_like(summary))
    _, carried = carried_in((restart, summary), "dp", combine, identity)
    gains = head_gain.reshape(heads_here, value_width)
    normed = finish(within, query_map, carried, request, starts, gains).reshape(
        row_count, heads_here * value_width
    )
    partial_terms = jnp.dot(
        normed,
        lax.all_gather(out_weight, "dp", axis=1, tiled=True),
        preferred_element_type=jnp.float32,
    )
    return lax.psum_scatter(
        partial_terms.astype(jnp.bfloat16), "mp", scatter_dimension=1, tiled=True
    )


def feature_tables(heads):
    first = np.zeros((heads, FEATS, heads * F), np.float32)
    second = np.zeros((heads, FEATS, heads * F), np.float32)
    scale = np.zeros((8, FEATS), np.float32)
    scale[0, 0] = scale[1, 0] = scale[2, 0] = scale[3, 0] = 1.0
    for a in range(F):
        first[np.arange(heads), 1 + a, np.arange(heads) * F + a] = 1.0
        scale[1, 1 + a] = 1.0
        scale[2, 1 + a] = scale[3, 1 + a] = 0.5
    for at, (a, b) in enumerate(SQUARES):
        row = 1 + F + at
        first[np.arange(heads), row, np.arange(heads) * F + a] = 1.0
        second[np.arange(heads), row, np.arange(heads) * F + b] = 1.0
        scale[2, row] = 0.25 / math.sqrt(2.0)
        scale[3, row] = (0.25 if a == b else 0.5) / math.sqrt(2.0)
    return first.astype(jnp.bfloat16), second.astype(jnp.bfloat16), scale


def chip(place, x):
    z, y = (place, 0) if place < 4 else (7 - place, 1)
    return z * 4 + y * 2 + x


def moves(step, flip):
    return [
        (chip(r, x), chip((r + step) % 8, x ^ flip)) for r in range(8) for x in range(2)
    ]


UP, DOWN, ACROSS = moves(1, 0), moves(-1, 0), moves(0, 1)


def ring_places():
    here = lax.axis_index("dp")
    z, y, x = here // 4, (here // 2) % 2, here % 2
    place = jnp.where(y == 0, z, 7 - z)
    there = (place + jnp.arange(8, dtype=jnp.int32)) % 8
    base = jnp.where(there < 4, there * 4, (7 - there) * 4 + 2)
    return jnp.concatenate([base + x, base + 1 - x]).astype(jnp.int32)


def send(value, pairs):
    return lax.ppermute(value, "dp", pairs)


def gather_rows(block):
    n = block.shape[0]
    h, q = n // 2, n // 4
    alone, pair = block[:h], block[h:]
    up1, down1, across = send(alone, UP), send(alone, DOWN), send(pair, ACROSS)
    both = jnp.concatenate([pair, across], axis=0)
    up2 = send(jnp.concatenate([both, up1], axis=0), UP)
    down2 = send(jnp.concatenate([both, down1], axis=0), DOWN)
    x1 = send(jnp.concatenate([alone, up1, down1], axis=0), ACROSS)
    up3, down3 = send(up2, UP), send(down2, DOWN)
    x2 = send(jnp.concatenate([up2[n:], down2[n:]], axis=0), ACROSS)
    up4 = send(up3[: n + q], UP)
    down4 = send(jnp.concatenate([down3[:n], down3[n + q :]], axis=0), DOWN)
    x3 = send(jnp.concatenate([up3[n:], down3[n:]], axis=0), ACROSS)
    up5, down5 = send(up4[:h], UP), send(down4[h:n], DOWN)
    x4 = send(jnp.concatenate([up4[n:], down4[n:]], axis=0), ACROSS)
    pieces = [
        (block, [(0, 0, n, 0)]),
        (across, [(8, h, h, 0)]),
        (up1, [(7, 0, h, 0)]),
        (down1, [(1, 0, h, 0)]),
        (x1, [(8, 0, h, 0), (15, 0, h, h), (9, 0, h, n)]),
        (up2, [(7, h, h, 0), (15, h, h, h), (6, 0, h, n)]),
        (down2, [(1, h, h, 0), (9, h, h, h), (2, 0, h, n)]),
        (x2, [(14, 0, h, 0), (10, 0, h, h)]),
        (up3, [(6, h, h, 0), (14, h, h, h), (5, 0, h, n)]),
        (down3, [(2, h, h, 0), (10, h, h, h), (3, 0, h, n)]),
        (x3, [(13, 0, h, 0), (11, 0, h, h)]),
        (up4, [(5, h, h, 0), (13, h, h, h), (4, 0, q, n)]),
        (down4, [(3, h, h, 0), (11, h, h, h), (4, q, q, n)]),
        (x4, [(12, 0, h, 0)]),
        (up5, [(4, h, h, 0)]),
        (down5, [(12, h, h, 0)]),
    ]
    return [piece for piece, _ in pieces], [places for _, places in pieces], up4


NT = (((1,), (1,)), ((), ()))


def project_kernel(layout, rows, heads, width, slots, tokens, low, up, tail, first, second, scale,
                   *refs):
    pieces, (query, keys, values, state, held) = refs[: len(layout)], refs[len(layout) :]
    for piece, places in zip(pieces, layout):
        for slot, row, count, source in places:
            at = pl.multiple_of(slots[slot] * rows + row, rows // 4)
            held[pl.ds(at, count), :] = piece[source : source + count, :]
    wide = heads * width
    small = heads * F
    both = jnp.dot(tokens[...], held[:, wide:], preferred_element_type=jnp.float32)
    query[...] = both[:, :small].astype(jnp.bfloat16)
    key_rows = both[:, small:].astype(jnp.bfloat16)
    keys[...] = key_rows
    for h in range(0, heads, 2):
        cols = slice(h * width, (h + 2) * width)
        total = jnp.dot(tokens[...], held[:, cols], preferred_element_type=jnp.float32)
        total += jnp.dot(low[...], up[:, cols], preferred_element_type=jnp.float32)
        values[:, cols] = total.astype(jnp.bfloat16)
        for g in (h, h + 1):
            a = lax.dot_general(first[g], key_rows, NT, preferred_element_type=jnp.float32)
            b = lax.dot_general(second[g], key_rows, NT, preferred_element_type=jnp.float32)
            mapped = ((a + scale[:, 0:1]) * (b + scale[:, 1:2])) * scale[:, 2:3]
            mapped = (mapped * tail[...]).astype(jnp.bfloat16)
            state[g] = jnp.dot(
                mapped, values[:, g * width : (g + 1) * width], preferred_element_type=jnp.float32
            ).astype(jnp.bfloat16)


def within_kernel(heads, width, query, keys, values, row, col, within):
    count = query.shape[0]
    cut = count // 2
    lanes = lax.broadcasted_iota(jnp.int32, (1, heads * F), 1)
    parts = ((0, cut), (cut, count))
    for low, high in parts:
        i = lax.broadcasted_iota(jnp.int32, (high - low, high), 0) + low
        j = lax.broadcasted_iota(jnp.int32, (high - low, high), 1)
        allowed = (j <= i) & (row[:, :high] == col[low:high, :])
        for h in range(heads):
            mine = jnp.where(lanes // F == h, 0.25, 0.0).astype(jnp.bfloat16)
            s = lax.dot_general(
                query[low:high, :] * mine, keys[:high, :], NT, preferred_element_type=jnp.float32
            )
            weights = 1.0 + s + 0.5 * s * s
            weights = jnp.where(allowed, weights, 0.0).astype(jnp.bfloat16)
            cols = slice(h * width, (h + 1) * width)
            within[low:high, cols] = jnp.dot(
                weights, values[:high, cols], preferred_element_type=jnp.float32
            )


def mix_kernel(blocks, marks, states, mixed):
    for b in range(blocks):
        total = jnp.zeros(states.shape[1:], jnp.float32)
        for e in range(b):
            total += marks[b * blocks + e] * states[e].astype(jnp.float32)
        mixed[b] = total.astype(jnp.bfloat16)


def finish_kernel(heads, width, within, query, carried, first, second, scale, follows, gains,
                  normed):
    rows = query[...]
    for h in range(heads):
        a = lax.dot_general(rows, first[h], NT, preferred_element_type=jnp.float32)
        b = lax.dot_general(rows, second[h], NT, preferred_element_type=jnp.float32)
        mapped = ((a + scale[0:1, :]) * (b + scale[1:2, :])) * scale[3:4, :]
        cross = jnp.dot(mapped.astype(jnp.bfloat16), carried[h], preferred_element_type=jnp.float32)
        cols = slice(h * width, (h + 1) * width)
        combined = within[:, cols] + follows[...] * cross
        factor = lax.rsqrt(jnp.mean(combined * combined, axis=-1, keepdims=True) + EPSILON)
        normed[:, cols] = (combined * factor * gains[:, cols]).astype(jnp.bfloat16)


def out_kernel(layout, tile, count, slots, which, normed, *refs):
    pieces, (theirs, mine, held, done) = refs[: len(layout)], refs[len(layout) :]
    copies = []
    for piece, places in zip(pieces, layout):
        for slot, row, rows, source in places:
            copies.append(
                pltpu.make_async_copy(
                    piece.at[pl.ds(source, rows)],
                    held.at[slots[slot], pl.ds(row, rows)],
                    done.at[len(copies)],
                )
            )
    for copy in copies:
        copy.start()
    for copy in copies:
        copy.wait()
    for out, half in ((theirs, 1 - which[0]), (mine, which[0])):
        for j in range(0, count // 2, 2):
            first = half * (count // 2) + j
            pair = jnp.concatenate([held[first], held[first + 1]], axis=1)
            out[:, j * tile : (j + 2) * tile] = jnp.dot(
                normed[...], pair, preferred_element_type=jnp.float32
            ).astype(out.dtype)


def per_device_fast(
    tokens,
    q_weight,
    k_weight,
    v_weight,
    adapter_down,
    adapter_up,
    lengths,
    adapter_ids,
    head_gain,
    out_weight,
):
    count, depth = tokens.shape
    blocks = lax.axis_size("dp")
    heads = q_weight.shape[1] // F
    width = v_weight.shape[1] // heads
    here, core = lax.axis_index("dp"), lax.axis_index("mp")
    params = pltpu.CompilerParams(vmem_limit_bytes=VMEM_LIMIT)

    positions = here * count + jnp.arange(count, dtype=jnp.int32)
    request, starts, adapter = token_tables(lengths, adapter_ids, positions)
    bounds = jnp.cumsum(lengths)
    opens = jnp.arange(blocks, dtype=jnp.int32) * count
    ends = opens + (count - 1)
    first_request = jnp.sum((opens[:, None] >= bounds[None, :]).astype(jnp.int32), axis=1)
    last_request = jnp.sum((ends[:, None] >= bounds[None, :]).astype(jnp.int32), axis=1)
    marks = (first_request[:, None] == last_request[None, :]).astype(jnp.float32).reshape(-1)
    tail = (request == request[-1]).astype(jnp.float32).reshape(1, count)
    follows = (request == request[0]).astype(jnp.float32).reshape(count, 1)

    other = lax.ppermute(adapter_down, "mp", [(0, 1), (1, 0)])
    wide = adapter_down.shape[1]
    owners = jnp.arange(wide, dtype=jnp.int32) // R
    lows = []
    for piece, place in ((adapter_down, core), (other, 1 - core)):
        partial = jnp.dot(tokens, piece, preferred_element_type=jnp.float32)
        kept = adapter[:, None] == owners[None, :] + place * (wide // R)
        lows.append(jnp.where(kept, partial, 0.0).astype(jnp.bfloat16))
    low = jnp.where(core == 0, jnp.concatenate(lows, 1), jnp.concatenate(lows[::-1], 1))

    first, second, scale = feature_tables(heads)
    first, second, scale = jnp.asarray(first), jnp.asarray(second), jnp.asarray(scale)

    rows = v_weight.shape[0]
    slots = ring_places()
    pieces, layout, late = gather_rows(jnp.concatenate([v_weight, q_weight, k_weight], axis=1))
    out_block, _ = lax.optimization_barrier((out_weight, late))
    out_pieces, out_layout, _ = gather_rows(out_block)
    total_width = heads * (width + 2 * F)
    query, keys, values, state = pl.pallas_call(
        functools.partial(project_kernel, layout, rows, heads, width),
        out_shape=(
            jax.ShapeDtypeStruct((count, heads * F), jnp.bfloat16),
            jax.ShapeDtypeStruct((count, heads * F), jnp.bfloat16),
            jax.ShapeDtypeStruct((count, heads * width), jnp.bfloat16),
            jax.ShapeDtypeStruct((heads, FEATS, width), jnp.bfloat16),
        ),
        in_specs=[SMEM] + [VMEM] * (7 + len(pieces)),
        out_specs=(VMEM,) * 4,
        scratch_shapes=[pltpu.VMEM((depth, total_width), jnp.bfloat16)],
        compiler_params=params,
        cost_estimate=pl.CostEstimate(
            flops=2 * count * depth * total_width, bytes_accessed=2 * depth * total_width * 2,
            transcendentals=0,
        ),
        name="project",
    )(slots, tokens, low, adapter_up, tail, first, second, scale.T, *pieces)

    parts = state.reshape(blocks, heads * FEATS // blocks, width)
    parts = lax.all_to_all(parts, "dp", 0, 0, tiled=True)
    mixed = pl.pallas_call(
        functools.partial(mix_kernel, blocks),
        out_shape=jax.ShapeDtypeStruct(parts.shape, jnp.bfloat16),
        in_specs=[SMEM, VMEM],
        out_specs=VMEM,
        compiler_params=params,
        name="mix",
    )(marks, parts)
    carried = lax.all_to_all(mixed, "dp", 0, 0, tiled=True).reshape(heads, FEATS, width)

    within = pl.pallas_call(
        functools.partial(within_kernel, heads, width),
        out_shape=jax.ShapeDtypeStruct((count, heads * width), jnp.float32),
        in_specs=[VMEM] * 5,
        out_specs=VMEM,
        compiler_params=params,
        cost_estimate=pl.CostEstimate(
            flops=4 * count * count * width * heads, bytes_accessed=4 * count * heads * width,
            transcendentals=0,
        ),
        name="within",
    )(query, keys, values, request.reshape(1, count), request.reshape(count, 1))

    normed = pl.pallas_call(
        functools.partial(finish_kernel, heads, width),
        out_shape=jax.ShapeDtypeStruct((count, heads * width), jnp.bfloat16),
        in_specs=[VMEM] * 8,
        out_specs=VMEM,
        compiler_params=params,
        cost_estimate=pl.CostEstimate(
            flops=4 * count * FEATS * width * heads, bytes_accessed=4 * count * heads * width,
            transcendentals=0,
        ),
        name="finish",
    )(within, query, carried, first, second, scale, follows, head_gain.reshape(1, -1))

    tile = out_weight.shape[1]
    held_shape = (blocks, heads * width, tile)
    theirs, mine = pl.pallas_call(
        functools.partial(out_kernel, out_layout, tile, blocks),
        out_shape=(
            jax.ShapeDtypeStruct((count, blocks * tile // 2), jnp.bfloat16),
            jax.ShapeDtypeStruct((count, blocks * tile // 2), jnp.float32),
        ),
        in_specs=[SMEM, SMEM, VMEM] + [ANY] * len(out_pieces),
        out_specs=(VMEM, VMEM),
        scratch_shapes=[
            pltpu.VMEM(held_shape, jnp.bfloat16),
            pltpu.SemaphoreType.DMA((sum(len(places) for places in out_layout),)),
        ],
        compiler_params=params,
        cost_estimate=pl.CostEstimate(
            flops=2 * count * heads * width * blocks * tile,
            bytes_accessed=4 * count * blocks * tile,
            transcendentals=0,
        ),
        name="out",
    )(slots, core.reshape(1).astype(jnp.int32), normed, *out_pieces)
    received = lax.ppermute(theirs, "mp", [(0, 1), (1, 0)])
    return (mine + received.astype(jnp.float32)).astype(jnp.bfloat16)


def solution(mesh):
    placed = (
        P("dp", None),
        P("dp", "mp"),
        P("dp", "mp"),
        P("dp", "mp"),
        P(None, "mp"),
        P(None, "mp"),
        P(),
        P(),
        P("mp"),
        P("mp", "dp"),
    )
    fast = mesh.shape["dp"] == 16 and mesh.shape["mp"] == 2
    return jax.shard_map(
        per_device_fast if fast else per_device_general,
        mesh=mesh,
        in_specs=placed,
        out_specs=P("dp", "mp"),
        check_vma=False,
    )
```

```python
import functools
import math

import jax
import jax.numpy as jnp
import numpy as np
from jax import lax
from jax.experimental import pallas as pl
from jax.experimental.pallas import tpu as pltpu
from jax.sharding import PartitionSpec as P

F = 16
R = 16
EPSILON = 1e-05
SQUARES = [(a, b) for a in range(F) for b in range(a, F)]
FEATS = 160
VMEM = pl.BlockSpec(memory_space=pltpu.VMEM)
SMEM = pl.BlockSpec(memory_space=pltpu.SMEM)
ANY = pl.BlockSpec(memory_space=pl.ANY)


def carried_in(value, axis, combine, identity):
    length, place = (lax.axis_size(axis), lax.axis_index(axis))
    everything = jax.tree.map(
        lambda part, kind: lax.all_gather(part.astype(kind), axis),
        value,
        (jnp.bfloat16, jnp.bfloat16),
    )
    start = jax.tree.map(
        lambda part, zero: jnp.broadcast_to(jnp.asarray(zero, part.dtype), part.shape),
        value,
        identity,
    )

    def turn(k, before):
        reached = k < place
        new = combine(
            before, jax.tree.map(lambda part, own: part[k].astype(own.dtype), everything, value)
        )
        return jax.tree.map(lambda a, b: jnp.where(reached, a, b), new, before)

    return lax.fori_loop(0, length, turn, start)


def taylor(inputs):
    squares = (inputs[..., :, None] * inputs[..., None, :]).reshape(
        inputs.shape[:-1] + (inputs.shape[-1] * inputs.shape[-1],)
    )
    constant = jnp.ones(inputs.shape[:-1] + (1,), jnp.float32)
    return jnp.concatenate([constant, 0.5 * inputs, squares * (0.25 / math.sqrt(2.0))], axis=-1)


def token_tables(lengths, adapter_ids, positions):
    bounds = jnp.cumsum(lengths)
    request = jnp.sum((positions[:, None] >= bounds[None, :]).astype(jnp.int32), axis=1)
    openings = bounds - lengths
    starts = jnp.any(positions[:, None] == openings[None, :], axis=1)
    picked = request[:, None] == jnp.arange(lengths.shape[0], dtype=jnp.int32)[None, :]
    adapter = jnp.sum(jnp.where(picked, adapter_ids[None, :], 0), axis=1)
    return (request, starts, adapter)


def block_local(query, key_rows, values, request, starts):
    scores = jnp.einsum("ihd,jhd->hij", query, key_rows, preferred_element_type=jnp.float32) * 0.25
    weights = 1.0 + scores + 0.5 * scores * scores
    indexes = jnp.arange(request.shape[0], dtype=jnp.int32)
    allowed = (indexes[None, :] <= indexes[:, None]) & (request[None, :] == request[:, None])
    weights = jnp.where(allowed[None], weights, 0.0).astype(jnp.bfloat16)
    within = jnp.einsum("hij,jhe->ihe", weights, values, preferred_element_type=jnp.float32)
    query_map = taylor(query.astype(jnp.float32)).astype(jnp.bfloat16)
    key_map = taylor(key_rows.astype(jnp.float32)).astype(jnp.bfloat16)
    tail_mask = (request == request[-1]).astype(jnp.bfloat16)
    masked_keys = key_map * tail_mask[:, None, None]
    summary = jnp.einsum("ihf,ihe->hfe", masked_keys, values, preferred_element_type=jnp.float32)
    restart = jnp.max(starts.astype(jnp.float32))
    return (within, query_map, summary, restart)


def finish(within, query_map, carried, request, starts, gains):
    follows = ((request == request[0]) & jnp.logical_not(starts[0])).astype(jnp.float32)
    cross = jnp.einsum(
        "ihf,hfe->ihe", query_map, carried.astype(jnp.bfloat16), preferred_element_type=jnp.float32
    )
    combined = within + follows[:, None, None] * cross
    factor = lax.rsqrt(jnp.mean(combined * combined, axis=-1, keepdims=True) + EPSILON)
    return (combined * factor * gains[None]).astype(jnp.bfloat16)


def combine(earlier, later):
    return (
        jnp.maximum(earlier[0], later[0]),
        jnp.where(later[0] > 0, later[1], earlier[1] + later[1]),
    )


def per_device_general(
    tokens,
    q_weight,
    k_weight,
    v_weight,
    adapter_down,
    adapter_up,
    lengths,
    adapter_ids,
    head_gain,
    out_weight,
):
    row_count = tokens.shape[0]
    heads_here = q_weight.shape[1] // F
    value_width = v_weight.shape[1] // heads_here
    positions = lax.axis_index("dp") * row_count + jnp.arange(row_count, dtype=jnp.int32)
    request, starts, adapter = token_tables(lengths, adapter_ids, positions)
    together = lax.all_gather(
        jnp.concatenate([q_weight, k_weight, v_weight], axis=1), "dp", axis=0, tiled=True
    )
    sums = jnp.dot(tokens, together, preferred_element_type=jnp.float32)
    width = heads_here * F
    query = sums[:, :width].astype(jnp.bfloat16).reshape(row_count, heads_here, F)
    key_rows = sums[:, width : 2 * width].astype(jnp.bfloat16).reshape(row_count, heads_here, F)
    value_sum = sums[:, 2 * width :]
    piece = lax.all_gather(adapter_down, "mp", axis=1, tiled=True)
    partial_low = jnp.dot(tokens, piece, preferred_element_type=jnp.float32)
    owners = jnp.arange(piece.shape[1], dtype=jnp.int32) // R
    low_rank = jnp.where(adapter[:, None] == owners[None, :], partial_low, 0.0).astype(jnp.bfloat16)
    values = value_sum + jnp.dot(low_rank, adapter_up, preferred_element_type=jnp.float32)
    values = values.astype(jnp.bfloat16).reshape(row_count, heads_here, value_width)
    within, query_map, summary, restart = block_local(query, key_rows, values, request, starts)
    identity = (jnp.zeros((), jnp.float32), jnp.zeros_like(summary))
    _, carried = carried_in((restart, summary), "dp", combine, identity)
    gains = head_gain.reshape(heads_here, value_width)
    normed = finish(within, query_map, carried, request, starts, gains).reshape(
        row_count, heads_here * value_width
    )
    partial_terms = jnp.dot(
        normed,
        lax.all_gather(out_weight, "dp", axis=1, tiled=True),
        preferred_element_type=jnp.float32,
    )
    return lax.psum_scatter(
        partial_terms.astype(jnp.bfloat16), "mp", scatter_dimension=1, tiled=True
    )


def feature_tables():
    first = np.zeros((FEATS, 128), np.float32)
    second = np.zeros((FEATS, 128), np.float32)
    scale = np.zeros((8, FEATS), np.float32)
    scale[:, 0] = 1.0
    for a in range(F):
        first[1 + a, a] = 1.0
        scale[1, 1 + a] = 1.0
        scale[2, 1 + a] = scale[3, 1 + a] = 0.5
    for at, (a, b) in enumerate(SQUARES):
        row = 1 + F + at
        first[row, a] = second[row, b] = 1.0
        scale[2, row] = 0.25 / math.sqrt(2.0)
        scale[3, row] = (0.25 if a == b else 0.5) / math.sqrt(2.0)
    return jnp.asarray(first), jnp.asarray(second), jnp.asarray(scale)


def table_of(table, head):
    turned = pltpu.roll(table[...], head * F, 1) if head else table[...]
    return turned.astype(jnp.bfloat16)


def chip(place, x):
    z, y = (place, 0) if place < 4 else (7 - place, 1)
    return z * 4 + y * 2 + x


def moves(step, flip):
    return [
        (chip(r, x), chip((r + step) % 8, x ^ flip)) for r in range(8) for x in range(2)
    ]


UP, DOWN, ACROSS = moves(1, 0), moves(-1, 0), moves(0, 1)


def place_of(here, slot):
    z, y, x = here // 4, (here // 2) % 2, here % 2
    there = (jnp.where(y == 0, z, 7 - z) + slot % 8) % 8
    base = jnp.where(there < 4, there * 4, (7 - there) * 4 + 2)
    return base + (x if slot < 8 else 1 - x)


def request_of(positions, lengths):
    bound, request = 0, jnp.zeros_like(positions)
    for k in range(lengths.shape[0]):
        bound = bound + lengths[k]
        request = request + jnp.where(positions >= bound, 1, 0)
    return request


def params(mebibytes):
    return pltpu.CompilerParams(vmem_limit_bytes=mebibytes * 1024 * 1024)


def send(value, pairs):
    return lax.ppermute(value, "dp", pairs)


def pack_kernel(recipes, sources, *refs):
    for recipe, out in zip(recipes, refs[len(refs) - len(recipes) :]):
        row = 0
        for source, start, rows in recipe:
            out[row : row + rows, :] = refs[source][start : start + rows, :]
            row += rows


def pack(recipes, sources, late=()):
    wide = sources[0].shape[1]
    return pl.pallas_call(
        functools.partial(pack_kernel, recipes, len(sources)),
        out_shape=[
            jax.ShapeDtypeStruct((sum(part[2] for part in recipe), wide), jnp.bfloat16)
            for recipe in recipes
        ],
        in_specs=[VMEM] * len(sources) + [ANY] * len(late),
        out_specs=[VMEM] * len(recipes),
        compiler_params=params(6),
        name="pack",
    )(*sources, *late)


def gather_rows(alone, pair):
    h = alone.shape[0]
    n, q = 2 * h, h // 2
    up1, down1, across = send(alone, UP), send(alone, DOWN), send(pair, ACROSS)
    late = yield up1, down1, across
    to_up, to_down, to_x = pack(
        [
            [(1, 0, h), (2, 0, h), (3, 0, h)],
            [(1, 0, h), (2, 0, h), (4, 0, h)],
            [(0, 0, h), (3, 0, h), (4, 0, h)],
        ],
        [alone, pair, across, up1, down1],
        late,
    )
    up2, down2, x1 = send(to_up, UP), send(to_down, DOWN), send(to_x, ACROSS)
    yield up2, down2, x1
    up3, down3 = send(up2, UP), send(down2, DOWN)
    (to_x,) = pack([[(0, n, h), (1, n, h)]], [up2, down2])
    x2 = send(to_x, ACROSS)
    late = yield up3, down3, x2
    to_up, to_down, to_x = pack(
        [[(0, 0, n + q)], [(1, 0, n), (1, n + q, q)], [(0, n, h), (1, n, h)]],
        [up3, down3],
        (x1,) + tuple(late),
    )
    up4, down4, x3 = send(to_up, UP), send(to_down, DOWN), send(to_x, ACROSS)
    late = yield up4, down4, x3
    to_up, to_down, to_x = pack(
        [[(0, 0, h)], [(1, h, h)], [(0, n, q), (1, n, q)]], [up4, down4], (x2,) + tuple(late)
    )
    up5, down5, x4 = send(to_up, UP), send(to_down, DOWN), send(to_x, ACROSS)
    yield up5, down5, x4
    yield [
        (alone, [(0, 0, h, 0)]),
        (pair, [(0, h, h, 0)]),
        (across, [(8, h, h, 0)]),
        (up1, [(7, 0, h, 0)]),
        (down1, [(1, 0, h, 0)]),
        (x1, [(8, 0, h, 0), (15, 0, h, h), (9, 0, h, n)]),
        (up2, [(7, h, h, 0), (15, h, h, h), (6, 0, h, n)]),
        (down2, [(1, h, h, 0), (9, h, h, h), (2, 0, h, n)]),
        (x2, [(14, 0, h, 0), (10, 0, h, h)]),
        (up3, [(6, h, h, 0), (14, h, h, h), (5, 0, h, n)]),
        (down3, [(2, h, h, 0), (10, h, h, h), (3, 0, h, n)]),
        (x3, [(13, 0, h, 0), (11, 0, h, h)]),
        (up4, [(5, h, h, 0), (13, h, h, h), (4, 0, q, n)]),
        (down4, [(3, h, h, 0), (11, h, h, h), (4, q, q, n)]),
        (x4, [(12, 0, h, 0)]),
        (up5, [(4, h, h, 0)]),
        (down5, [(12, h, h, 0)]),
    ]


def piece_rows(pieces, layout, slot, row, rows, cols=slice(None)):
    found = []
    while rows:
        for piece, places in zip(pieces, layout):
            for at, first, count, source in places:
                if at == slot and first <= row < first + count and rows:
                    take = min(rows, first + count - row)
                    start = source + row - first
                    found.append(piece[start : start + take, cols])
                    row, rows = row + take, rows - take
    return found[0] if len(found) == 1 else jnp.concatenate(found, axis=0)


NT = (((1,), (1,)), ((), ()))


def join_kernel(values, query, keys, alone, pair, done):
    half, wide = alone.shape[0], values.shape[1]
    small = query.shape[1]
    copies = []
    for out, row in ((alone, 0), (pair, half)):
        for source, at in ((values, 0), (query, wide), (keys, wide + small)):
            copies.append(
                pltpu.make_async_copy(
                    source.at[pl.ds(row, half)],
                    out.at[:, pl.ds(at, source.shape[1])],
                    done.at[len(copies)],
                )
            )
    for copy in copies:
        copy.start()
    for copy in copies:
        copy.wait()


def join(values, query, keys):
    rows, wide = values.shape[0], values.shape[1] + query.shape[1] + keys.shape[1]
    return pl.pallas_call(
        join_kernel,
        out_shape=[jax.ShapeDtypeStruct((rows // 2, wide), values.dtype)] * 2,
        in_specs=[ANY] * 3,
        out_specs=[VMEM] * 2,
        scratch_shapes=[pltpu.SemaphoreType.DMA((6,))],
        compiler_params=params(4),
        name="join",
    )(values, query, keys)


def turn_kernel(rows, info, tokens, turned):
    for slot in range(tokens.shape[1] // rows):
        source = pl.ds(pl.multiple_of(place_of(info[0], slot) * rows, rows), rows)
        turned[:, slot * rows : (slot + 1) * rows] = tokens[:, source]


def low_kernel(info, lengths, adapter_ids, tokens, own, other, low):
    count, wide = tokens.shape[0], own.shape[1]
    positions = lax.broadcasted_iota(jnp.int32, (count, 1), 0) + info[0] * count
    request = request_of(positions, lengths)
    adapter = jnp.zeros_like(request)
    for k in range(lengths.shape[0]):
        adapter = jnp.where(request == k, adapter_ids[k], adapter)
    owners = lax.broadcasted_iota(jnp.int32, (1, wide), 1) // R
    for piece, place in ((own, info[1]), (other, 1 - info[1])):
        partial = jnp.dot(tokens[...], piece[...], preferred_element_type=jnp.float32)
        kept = adapter == owners + place * (wide // R)
        cols = pl.ds(pl.multiple_of(place * wide, wide), wide)
        low[:, cols] = jnp.where(kept, partial, 0.0).astype(jnp.bfloat16)


def project_kernel(layout, rows, heads, width, info, lengths, tokens, low, up, first, second,
                   scale, *refs):
    pieces, (query, keys, values, state) = refs[: len(layout)], refs[len(layout) :]
    count, depth = tokens.shape
    wide = heads * width
    small = heads * F

    def product(cols):
        total = None
        for slot in range(0, depth // rows, 2):
            weight = jnp.concatenate(
                [piece_rows(pieces, layout, at, 0, rows, cols) for at in (slot, slot + 1)], axis=0
            )
            term = jnp.dot(
                tokens[:, slot * rows : (slot + 2) * rows], weight,
                preferred_element_type=jnp.float32,
            )
            total = term if total is None else total + term
        return total

    both = product(slice(wide, wide + 2 * small))
    query[...] = both[:, :small].astype(jnp.bfloat16)
    key_rows = both[:, small:].astype(jnp.bfloat16)
    keys[...] = key_rows
    positions = lax.broadcasted_iota(jnp.int32, (1, count), 1) + info[0] * count
    end = request_of(jnp.full((1, 1), count - 1, jnp.int32) + info[0] * count, lengths)
    tail = jnp.where(request_of(positions, lengths) == end, 1.0, 0.0)
    maps = []
    for h in range(heads):
        a = lax.dot_general(table_of(first, h), key_rows, NT, preferred_element_type=jnp.float32)
        b = lax.dot_general(table_of(second, h), key_rows, NT, preferred_element_type=jnp.float32)
        mapped = ((a + scale[:, 0:1]) * (b + scale[:, 1:2])) * scale[:, 2:3]
        maps.append((mapped * tail).astype(jnp.bfloat16))
    for h in range(0, heads, 2):
        cols = slice(h * width, (h + 2) * width)
        total = product(cols)
        total += jnp.dot(low[...], up[:, cols], preferred_element_type=jnp.float32)
        values[:, cols] = total.astype(jnp.bfloat16)
    for h in range(heads):
        state[h] = jnp.dot(
            maps[h], values[:, h * width : (h + 1) * width], preferred_element_type=jnp.float32
        ).astype(jnp.bfloat16)


def within_kernel(heads, width, info, lengths, query, keys, values, first, second, scale, within,
                  maps):
    count = query.shape[0]
    cut = count // 2
    lanes = lax.broadcasted_iota(jnp.int32, (1, heads * F), 1)
    start = info[0] * count
    row = request_of(lax.broadcasted_iota(jnp.int32, (1, count), 1) + start, lengths)
    col = request_of(lax.broadcasted_iota(jnp.int32, (count, 1), 0) + start, lengths)
    for low, high in ((0, cut), (cut, count)):
        i = lax.broadcasted_iota(jnp.int32, (high - low, high), 0) + low
        j = lax.broadcasted_iota(jnp.int32, (high - low, high), 1)
        allowed = (j <= i) & (row[:, :high] == col[low:high, :])
        for h in range(heads):
            mine = jnp.where(lanes // F == h, 0.25, 0.0).astype(jnp.bfloat16)
            s = lax.dot_general(
                query[low:high, :] * mine, keys[:high, :], NT, preferred_element_type=jnp.float32
            )
            weights = 1.0 + s + 0.5 * s * s
            weights = jnp.where(allowed, weights, 0.0).astype(jnp.bfloat16)
            cols = slice(h * width, (h + 1) * width)
            within[low:high, cols] = jnp.dot(
                weights, values[:high, cols], preferred_element_type=jnp.float32
            )
    for h in range(heads):
        a = lax.dot_general(query[...], table_of(first, h), NT, preferred_element_type=jnp.float32)
        b = lax.dot_general(query[...], table_of(second, h), NT, preferred_element_type=jnp.float32)
        mapped = ((a + scale[0:1, :]) * (b + scale[1:2, :])) * scale[3:4, :]
        maps[h] = mapped.astype(jnp.bfloat16)


def mix_kernel(blocks, count, lengths, states, mixed):
    def request(position):
        bound, found = 0, 0
        for k in range(lengths.shape[0]):
            bound = bound + lengths[k]
            found = found + jnp.where(position >= bound, 1, 0)
        return found

    begin = [request(b * count) for b in range(blocks)]
    end = [request((b + 1) * count - 1) for b in range(blocks)]
    total = jnp.zeros(states.shape[1:], jnp.float32)
    mixed[0] = total.astype(jnp.bfloat16)
    for b in range(1, blocks):
        whole = jnp.where(begin[b - 1] == end[b - 1], 1.0, 0.0)
        goes_on = jnp.where(end[b - 1] == begin[b], 1.0, 0.0)
        total = (states[b - 1].astype(jnp.float32) + whole * total) * goes_on
        mixed[b] = total.astype(jnp.bfloat16)


def finish_kernel(heads, width, info, lengths, within, maps, carried, gains, normed):
    count = within.shape[0]
    positions = lax.broadcasted_iota(jnp.int32, (count, 1), 0) + info[0] * count
    begin = request_of(jnp.zeros((1, 1), jnp.int32) + info[0] * count, lengths)
    follows = jnp.where(request_of(positions, lengths) == begin, 1.0, 0.0)
    for h in range(heads):
        cross = jnp.dot(maps[h], carried[h], preferred_element_type=jnp.float32)
        cols = slice(h * width, (h + 1) * width)
        combined = within[:, cols] + follows * cross
        factor = lax.rsqrt(jnp.mean(combined * combined, axis=-1, keepdims=True) + EPSILON)
        normed[:, cols] = (combined * factor * gains[:, cols]).astype(jnp.bfloat16)


def out_kernel(layout, tile, blocks, info, normed, *refs):
    pieces, (out,) = refs[: len(layout)], refs[len(layout) :]
    depth = normed.shape[1]
    step = depth // 4
    for near in range(blocks // 2):
        pair = (near, near + blocks // 2)
        total = None
        for row in range(0, depth, step):
            both = jnp.concatenate(
                [piece_rows(pieces, layout, slot, row, step) for slot in pair], axis=1
            )
            term = jnp.dot(normed[:, row : row + step], both, preferred_element_type=jnp.float32)
            total = term if total is None else total + term
        for k, slot in enumerate(pair):
            place = place_of(info[0], slot)
            at = jnp.where(place // (blocks // 2) == info[1], 0, blocks // 2) + place % (blocks // 2)
            out[at] = total[:, k * tile : (k + 1) * tile].astype(jnp.bfloat16)


def add_kernel(partial, received, out):
    tile = partial.shape[2]
    for k in range(received.shape[0]):
        total = partial[k].astype(jnp.float32) + received[k].astype(jnp.float32)
        out[:, k * tile : (k + 1) * tile] = total.astype(jnp.bfloat16)


def call(kernel, name, mebibytes, cost, shapes, scalars, arrays, late=()):
    shapes = [jax.ShapeDtypeStruct(shape, kind) for shape, kind in shapes]
    given = len(scalars) + len(arrays)

    def body(*refs):
        kernel(*refs[:given], *refs[given + len(late) :])

    return pl.pallas_call(
        body,
        out_shape=shapes,
        in_specs=[SMEM] * len(scalars) + [VMEM] * len(arrays) + [ANY] * len(late),
        out_specs=[VMEM] * len(shapes),
        compiler_params=params(mebibytes),
        cost_estimate=pl.CostEstimate(flops=cost[0], bytes_accessed=cost[1], transcendentals=0),
        name=name,
    )(*scalars, *arrays, *late)


def per_device_fast(
    tokens,
    q_weight,
    k_weight,
    v_weight,
    adapter_down,
    adapter_up,
    lengths,
    adapter_ids,
    head_gain,
    out_weight,
):
    count, depth = tokens.shape
    blocks = lax.axis_size("dp")
    heads = q_weight.shape[1] // F
    width = v_weight.shape[1] // heads
    rows = v_weight.shape[0]
    wide, small, total = heads * width, heads * F, heads * (width + 2 * F)
    tile = out_weight.shape[1]
    half = jnp.bfloat16
    info = jnp.stack([lax.axis_index("dp"), lax.axis_index("mp")]).astype(jnp.int32)
    first, second, scale = feature_tables()

    alone, pair = join(v_weight, q_weight, k_weight)
    other = lax.ppermute(adapter_down, "mp", [(0, 1), (1, 0)])
    (turned,) = call(
        functools.partial(turn_kernel, rows), "turn", 8, (0, 4 * count * depth),
        [((count, depth), half)], [info], [tokens],
    )
    (low,) = call(
        low_kernel, "low", 8, (4 * count * depth * adapter_down.shape[1], 2 * count * depth),
        [((count, 2 * adapter_down.shape[1]), half)], [info, lengths, adapter_ids],
        [tokens, adapter_down, other],
    )

    chain = gather_rows(alone, pair)
    next(chain)
    second_round = chain.send(())
    third = next(chain)
    out_alone, out_pair = pack(
        [[(0, 0, wide // 2)], [(0, wide // 2, wide // 2)]], [out_weight], second_round[:2]
    )
    out_chain = gather_rows(out_alone, out_pair)
    out_first = next(out_chain)
    chain.send((turned, low) + out_first)
    out_second = out_chain.send(third[:2])
    fifth = chain.send(())
    gathered = next(chain)
    out_third = next(out_chain)

    pieces, layout = [piece for piece, _ in gathered], [places for _, places in gathered]
    query, keys, values, state = call(
        functools.partial(project_kernel, layout, rows, heads, width), "project", 14,
        (2 * count * depth * total, 2 * depth * total),
        [
            ((count, small), half),
            ((count, small), half),
            ((count, wide), half),
            ((heads, FEATS, width), half),
        ],
        [info, lengths], [turned, low, adapter_up, first, second, scale.T, *pieces],
    )
    parts = state.reshape(blocks, heads * FEATS // blocks, width)
    parts = lax.all_to_all(parts, "dp", 0, 0, tiled=True)
    out_fourth = out_chain.send(())
    out_chain.send(())
    out_gathered = next(out_chain)
    (mixed,) = call(
        functools.partial(mix_kernel, blocks, count), "mix", 4, (0, 4 * parts.size),
        [(parts.shape, half)], [lengths], [parts], out_third[:2],
    )
    carried = lax.all_to_all(mixed, "dp", 0, 0, tiled=True).reshape(heads, FEATS, width)
    within, maps = call(
        functools.partial(within_kernel, heads, width), "within", 12,
        (4 * count * count * wide, 8 * count * wide),
        [((count, wide), jnp.float32), ((heads, count, FEATS), half)],
        [info, lengths], [query, keys, values, first, second, scale],
    )
    (normed,) = call(
        functools.partial(finish_kernel, heads, width), "finish", 10,
        (2 * count * FEATS * wide, 8 * count * wide), [((count, wide), half)],
        [info, lengths],
        [within, maps, carried, head_gain.reshape(1, -1)], out_fourth[:2],
    )
    pieces, layout = [piece for piece, _ in out_gathered], [places for _, places in out_gathered]
    (partial,) = call(
        functools.partial(out_kernel, layout, tile, blocks), "out", 12,
        (2 * count * wide * blocks * tile, 4 * count * blocks * tile),
        [((blocks, count, tile), half)], [info], [normed, *pieces],
    )
    received = lax.ppermute(partial[blocks // 2 :], "mp", [(0, 1), (1, 0)])
    (result,) = call(
        add_kernel, "add", 8, (0, 8 * count * wide), [((count, blocks // 2 * tile), half)], [],
        [partial, received],
    )
    return result


def solution(mesh):
    placed = (
        P("dp", None),
        P("dp", "mp"),
        P("dp", "mp"),
        P("dp", "mp"),
        P(None, "mp"),
        P(None, "mp"),
        P(),
        P(),
        P("mp"),
        P("mp", "dp"),
    )
    fast = mesh.shape["dp"] == 16 and mesh.shape["mp"] == 2
    return jax.shard_map(
        per_device_fast if fast else per_device_general,
        mesh=mesh,
        in_specs=placed,
        out_specs=P("dp", "mp"),
        check_vma=False,
    )
```

```python
import functools
import math

import jax
import jax.numpy as jnp
import numpy as np
from jax import lax
from jax.experimental import pallas as pl
from jax.experimental.pallas import tpu as pltpu
from jax.sharding import PartitionSpec as P

F = 16
R = 16
EPSILON = 1e-05
SQUARES = [(a, b) for a in range(F) for b in range(a, F)]
FEATS = 160
VMEM = pl.BlockSpec(memory_space=pltpu.VMEM)
SMEM = pl.BlockSpec(memory_space=pltpu.SMEM)
ANY = pl.BlockSpec(memory_space=pl.ANY)
HBM = pl.BlockSpec(memory_space=pltpu.HBM)


def carried_in(value, axis, combine, identity):
    length, place = (lax.axis_size(axis), lax.axis_index(axis))
    everything = jax.tree.map(
        lambda part, kind: lax.all_gather(part.astype(kind), axis),
        value,
        (jnp.bfloat16, jnp.bfloat16),
    )
    start = jax.tree.map(
        lambda part, zero: jnp.broadcast_to(jnp.asarray(zero, part.dtype), part.shape),
        value,
        identity,
    )

    def turn(k, before):
        reached = k < place
        new = combine(
            before, jax.tree.map(lambda part, own: part[k].astype(own.dtype), everything, value)
        )
        return jax.tree.map(lambda a, b: jnp.where(reached, a, b), new, before)

    return lax.fori_loop(0, length, turn, start)


def taylor(inputs):
    squares = (inputs[..., :, None] * inputs[..., None, :]).reshape(
        inputs.shape[:-1] + (inputs.shape[-1] * inputs.shape[-1],)
    )
    constant = jnp.ones(inputs.shape[:-1] + (1,), jnp.float32)
    return jnp.concatenate([constant, 0.5 * inputs, squares * (0.25 / math.sqrt(2.0))], axis=-1)


def token_tables(lengths, adapter_ids, positions):
    bounds = jnp.cumsum(lengths)
    request = jnp.sum((positions[:, None] >= bounds[None, :]).astype(jnp.int32), axis=1)
    openings = bounds - lengths
    starts = jnp.any(positions[:, None] == openings[None, :], axis=1)
    picked = request[:, None] == jnp.arange(lengths.shape[0], dtype=jnp.int32)[None, :]
    adapter = jnp.sum(jnp.where(picked, adapter_ids[None, :], 0), axis=1)
    return (request, starts, adapter)


def block_local(query, key_rows, values, request, starts):
    scores = jnp.einsum("ihd,jhd->hij", query, key_rows, preferred_element_type=jnp.float32) * 0.25
    weights = 1.0 + scores + 0.5 * scores * scores
    indexes = jnp.arange(request.shape[0], dtype=jnp.int32)
    allowed = (indexes[None, :] <= indexes[:, None]) & (request[None, :] == request[:, None])
    weights = jnp.where(allowed[None], weights, 0.0).astype(jnp.bfloat16)
    within = jnp.einsum("hij,jhe->ihe", weights, values, preferred_element_type=jnp.float32)
    query_map = taylor(query.astype(jnp.float32)).astype(jnp.bfloat16)
    key_map = taylor(key_rows.astype(jnp.float32)).astype(jnp.bfloat16)
    tail_mask = (request == request[-1]).astype(jnp.bfloat16)
    masked_keys = key_map * tail_mask[:, None, None]
    summary = jnp.einsum("ihf,ihe->hfe", masked_keys, values, preferred_element_type=jnp.float32)
    restart = jnp.max(starts.astype(jnp.float32))
    return (within, query_map, summary, restart)


def finish(within, query_map, carried, request, starts, gains):
    follows = ((request == request[0]) & jnp.logical_not(starts[0])).astype(jnp.float32)
    cross = jnp.einsum(
        "ihf,hfe->ihe", query_map, carried.astype(jnp.bfloat16), preferred_element_type=jnp.float32
    )
    combined = within + follows[:, None, None] * cross
    factor = lax.rsqrt(jnp.mean(combined * combined, axis=-1, keepdims=True) + EPSILON)
    return (combined * factor * gains[None]).astype(jnp.bfloat16)


def combine(earlier, later):
    return (
        jnp.maximum(earlier[0], later[0]),
        jnp.where(later[0] > 0, later[1], earlier[1] + later[1]),
    )


def per_device_general(
    tokens,
    q_weight,
    k_weight,
    v_weight,
    adapter_down,
    adapter_up,
    lengths,
    adapter_ids,
    head_gain,
    out_weight,
):
    row_count = tokens.shape[0]
    heads_here = q_weight.shape[1] // F
    value_width = v_weight.shape[1] // heads_here
    positions = lax.axis_index("dp") * row_count + jnp.arange(row_count, dtype=jnp.int32)
    request, starts, adapter = token_tables(lengths, adapter_ids, positions)
    together = lax.all_gather(
        jnp.concatenate([q_weight, k_weight, v_weight], axis=1), "dp", axis=0, tiled=True
    )
    sums = jnp.dot(tokens, together, preferred_element_type=jnp.float32)
    width = heads_here * F
    query = sums[:, :width].astype(jnp.bfloat16).reshape(row_count, heads_here, F)
    key_rows = sums[:, width : 2 * width].astype(jnp.bfloat16).reshape(row_count, heads_here, F)
    value_sum = sums[:, 2 * width :]
    piece = lax.all_gather(adapter_down, "mp", axis=1, tiled=True)
    partial_low = jnp.dot(tokens, piece, preferred_element_type=jnp.float32)
    owners = jnp.arange(piece.shape[1], dtype=jnp.int32) // R
    low_rank = jnp.where(adapter[:, None] == owners[None, :], partial_low, 0.0).astype(jnp.bfloat16)
    values = value_sum + jnp.dot(low_rank, adapter_up, preferred_element_type=jnp.float32)
    values = values.astype(jnp.bfloat16).reshape(row_count, heads_here, value_width)
    within, query_map, summary, restart = block_local(query, key_rows, values, request, starts)
    identity = (jnp.zeros((), jnp.float32), jnp.zeros_like(summary))
    _, carried = carried_in((restart, summary), "dp", combine, identity)
    gains = head_gain.reshape(heads_here, value_width)
    normed = finish(within, query_map, carried, request, starts, gains).reshape(
        row_count, heads_here * value_width
    )
    partial_terms = jnp.dot(
        normed,
        lax.all_gather(out_weight, "dp", axis=1, tiled=True),
        preferred_element_type=jnp.float32,
    )
    return lax.psum_scatter(
        partial_terms.astype(jnp.bfloat16), "mp", scatter_dimension=1, tiled=True
    )


def feature_tables():
    first = np.zeros((FEATS, 128), np.float32)
    second = np.zeros((FEATS, 128), np.float32)
    scale = np.zeros((8, FEATS), np.float32)
    scale[:, 0] = 1.0
    for a in range(F):
        first[1 + a, a] = 1.0
        scale[1, 1 + a] = 1.0
        scale[2, 1 + a] = scale[3, 1 + a] = 0.5
    for at, (a, b) in enumerate(SQUARES):
        row = 1 + F + at
        first[row, a] = second[row, b] = 1.0
        scale[2, row] = 0.25 / math.sqrt(2.0)
        scale[3, row] = (0.25 if a == b else 0.5) / math.sqrt(2.0)
    return jnp.asarray(first), jnp.asarray(second), jnp.asarray(scale)


def table_of(table, head):
    turned = pltpu.roll(table[...], head * F, 1) if head else table[...]
    return turned.astype(jnp.bfloat16)


def chip(place, x):
    z, y = (place, 0) if place < 4 else (7 - place, 1)
    return z * 4 + y * 2 + x


def moves(step, flip):
    return [
        (chip(r, x), chip((r + step) % 8, x ^ flip)) for r in range(8) for x in range(2)
    ]


UP, DOWN, ACROSS = moves(1, 0), moves(-1, 0), moves(0, 1)


def place_of(here, slot):
    z, y, x = here // 4, (here // 2) % 2, here % 2
    there = (jnp.where(y == 0, z, 7 - z) + slot % 8) % 8
    base = jnp.where(there < 4, there * 4, (7 - there) * 4 + 2)
    return base + (x if slot < 8 else 1 - x)


def request_of(positions, lengths):
    bound, request = 0, jnp.zeros_like(positions)
    for k in range(lengths.shape[0]):
        bound = bound + lengths[k]
        request = request + jnp.where(positions >= bound, 1, 0)
    return request


def params(mebibytes):
    return pltpu.CompilerParams(vmem_limit_bytes=mebibytes * 1024 * 1024)


def send(value, pairs):
    return lax.ppermute(value, "dp", pairs)


def pack_kernel(recipes, sources, *refs):
    for recipe, out in zip(recipes, refs[len(refs) - len(recipes) :]):
        row = 0
        for source, start, rows in recipe:
            out[row : row + rows, :] = refs[source][start : start + rows, :]
            row += rows


def pack(recipes, sources, late=()):
    wide = sources[0].shape[1]
    return pl.pallas_call(
        functools.partial(pack_kernel, recipes, len(sources)),
        out_shape=[
            jax.ShapeDtypeStruct((sum(part[2] for part in recipe), wide), jnp.bfloat16)
            for recipe in recipes
        ],
        in_specs=[VMEM] * len(sources) + [ANY] * len(late),
        out_specs=[VMEM] * len(recipes),
        compiler_params=params(6),
        name="pack",
    )(*sources, *late)


def gather_rows(alone, pair):
    h = alone.shape[0]
    n, q = 2 * h, h // 2
    up1, down1, across = send(alone, UP), send(alone, DOWN), send(pair, ACROSS)
    late = yield up1, down1, across
    to_up, to_down, to_x = pack(
        [
            [(1, 0, h), (2, 0, h), (3, 0, h)],
            [(1, 0, h), (2, 0, h), (4, 0, h)],
            [(0, 0, h), (3, 0, h), (4, 0, h)],
        ],
        [alone, pair, across, up1, down1],
        late,
    )
    up2, down2, x1 = send(to_up, UP), send(to_down, DOWN), send(to_x, ACROSS)
    yield up2, down2, x1
    up3, down3 = send(up2, UP), send(down2, DOWN)
    (to_x,) = pack([[(0, n, h), (1, n, h)]], [up2, down2])
    x2 = send(to_x, ACROSS)
    late = yield up3, down3, x2
    to_up, to_down, to_x = pack(
        [[(0, 0, n + q)], [(1, 0, n), (1, n + q, q)], [(0, n, h), (1, n, h)]],
        [up3, down3],
        (x1,) + tuple(late),
    )
    up4, down4, x3 = send(to_up, UP), send(to_down, DOWN), send(to_x, ACROSS)
    late = yield up4, down4, x3
    to_up, to_down, to_x = pack(
        [[(0, 0, h)], [(1, h, h)], [(0, n, q), (1, n, q)]], [up4, down4], (x2,) + tuple(late)
    )
    up5, down5, x4 = send(to_up, UP), send(to_down, DOWN), send(to_x, ACROSS)
    yield up5, down5, x4
    yield [
        (alone, [(0, 0, h, 0)]),
        (pair, [(0, h, h, 0)]),
        (across, [(8, h, h, 0)]),
        (up1, [(7, 0, h, 0)]),
        (down1, [(1, 0, h, 0)]),
        (x1, [(8, 0, h, 0), (15, 0, h, h), (9, 0, h, n)]),
        (up2, [(7, h, h, 0), (15, h, h, h), (6, 0, h, n)]),
        (down2, [(1, h, h, 0), (9, h, h, h), (2, 0, h, n)]),
        (x2, [(14, 0, h, 0), (10, 0, h, h)]),
        (up3, [(6, h, h, 0), (14, h, h, h), (5, 0, h, n)]),
        (down3, [(2, h, h, 0), (10, h, h, h), (3, 0, h, n)]),
        (x3, [(13, 0, h, 0), (11, 0, h, h)]),
        (up4, [(5, h, h, 0), (13, h, h, h), (4, 0, q, n)]),
        (down4, [(3, h, h, 0), (11, h, h, h), (4, q, q, n)]),
        (x4, [(12, 0, h, 0)]),
        (up5, [(4, h, h, 0)]),
        (down5, [(12, h, h, 0)]),
    ]


def piece_rows(pieces, layout, slot, row, rows, cols=slice(None)):
    found = []
    while rows:
        for piece, places in zip(pieces, layout):
            for at, first, count, source in places:
                if at == slot and first <= row < first + count and rows:
                    take = min(rows, first + count - row)
                    start = source + row - first
                    found.append(piece[start : start + take, cols])
                    row, rows = row + take, rows - take
    return found[0] if len(found) == 1 else jnp.concatenate(found, axis=0)


NT = (((1,), (1,)), ((), ()))


def join_kernel(values, query, keys, alone, pair, done):
    half, wide = alone.shape[0], values.shape[1]
    small = query.shape[1]
    copies = []
    for out, row in ((alone, 0), (pair, half)):
        for source, at in ((values, 0), (query, wide), (keys, wide + small)):
            copies.append(
                pltpu.make_async_copy(
                    source.at[pl.ds(row, half)],
                    out.at[:, pl.ds(at, source.shape[1])],
                    done.at[len(copies)],
                )
            )
    for copy in copies:
        copy.start()
    for copy in copies:
        copy.wait()


def join(values, query, keys):
    rows, wide = values.shape[0], values.shape[1] + query.shape[1] + keys.shape[1]
    return pl.pallas_call(
        join_kernel,
        out_shape=[jax.ShapeDtypeStruct((rows // 2, wide), values.dtype)] * 2,
        in_specs=[HBM] * 3,
        out_specs=[VMEM] * 2,
        scratch_shapes=[pltpu.SemaphoreType.DMA((6,))],
        compiler_params=params(4),
        name="join",
    )(stay(values), stay(query), stay(keys))


def turn_kernel(rows, info, tokens, turned):
    for slot in range(tokens.shape[1] // rows):
        source = pl.ds(pl.multiple_of(place_of(info[0], slot) * rows, rows), rows)
        turned[:, slot * rows : (slot + 1) * rows] = tokens[:, source]


def low_kernel(info, lengths, adapter_ids, tokens, own, other, low):
    count, wide = tokens.shape[0], own.shape[1]
    positions = lax.broadcasted_iota(jnp.int32, (count, 1), 0) + info[0] * count
    request = request_of(positions, lengths)
    adapter = jnp.zeros_like(request)
    for k in range(lengths.shape[0]):
        adapter = jnp.where(request == k, adapter_ids[k], adapter)
    owners = lax.broadcasted_iota(jnp.int32, (1, wide), 1) // R
    for piece, place in ((own, info[1]), (other, 1 - info[1])):
        partial = jnp.dot(tokens[...], piece[...], preferred_element_type=jnp.float32)
        kept = adapter == owners + place * (wide // R)
        cols = pl.ds(pl.multiple_of(place * wide, wide), wide)
        low[:, cols] = jnp.where(kept, partial, 0.0).astype(jnp.bfloat16)


def project_kernel(layout, rows, heads, width, info, lengths, tokens, low, up, first, second,
                   scale, *refs):
    pieces, (query, keys, values, state) = refs[: len(layout)], refs[len(layout) :]
    count, depth = tokens.shape
    wide = heads * width
    small = heads * F

    def product(cols):
        total = None
        for slot in range(0, depth // rows, 2):
            weight = jnp.concatenate(
                [piece_rows(pieces, layout, at, 0, rows, cols) for at in (slot, slot + 1)], axis=0
            )
            term = jnp.dot(
                tokens[:, slot * rows : (slot + 2) * rows], weight,
                preferred_element_type=jnp.float32,
            )
            total = term if total is None else total + term
        return total

    both = product(slice(wide, wide + 2 * small))
    query[...] = both[:, :small].astype(jnp.bfloat16)
    key_rows = both[:, small:].astype(jnp.bfloat16)
    keys[...] = key_rows
    positions = lax.broadcasted_iota(jnp.int32, (1, count), 1) + info[0] * count
    end = request_of(jnp.full((1, 1), count - 1, jnp.int32) + info[0] * count, lengths)
    tail = jnp.where(request_of(positions, lengths) == end, 1.0, 0.0)
    maps = []
    for h in range(heads):
        a = lax.dot_general(table_of(first, h), key_rows, NT, preferred_element_type=jnp.float32)
        b = lax.dot_general(table_of(second, h), key_rows, NT, preferred_element_type=jnp.float32)
        mapped = ((a + scale[:, 0:1]) * (b + scale[:, 1:2])) * scale[:, 2:3]
        maps.append((mapped * tail).astype(jnp.bfloat16))
    for h in range(0, heads, 2):
        cols = slice(h * width, (h + 2) * width)
        total = product(cols)
        total += jnp.dot(low[...], up[:, cols], preferred_element_type=jnp.float32)
        values[:, cols] = total.astype(jnp.bfloat16)
    for h in range(heads):
        state[h] = jnp.dot(
            maps[h], values[:, h * width : (h + 1) * width], preferred_element_type=jnp.float32
        ).astype(jnp.bfloat16)


def within_kernel(heads, width, info, lengths, query, keys, values, within):
    count = query.shape[0]
    cut = count // 2
    lanes = lax.broadcasted_iota(jnp.int32, (1, heads * F), 1)
    start = info[0] * count
    row = request_of(lax.broadcasted_iota(jnp.int32, (1, count), 1) + start, lengths)
    col = request_of(lax.broadcasted_iota(jnp.int32, (count, 1), 0) + start, lengths)
    for low, high in ((0, cut), (cut, count)):
        i = lax.broadcasted_iota(jnp.int32, (high - low, high), 0) + low
        j = lax.broadcasted_iota(jnp.int32, (high - low, high), 1)
        allowed = (j <= i) & (row[:, :high] == col[low:high, :])
        for h in range(heads):
            mine = jnp.where(lanes // F == h, 0.25, 0.0).astype(jnp.bfloat16)
            s = lax.dot_general(
                query[low:high, :] * mine, keys[:high, :], NT, preferred_element_type=jnp.float32
            )
            weights = 1.0 + s + 0.5 * s * s
            weights = jnp.where(allowed, weights, 0.0).astype(jnp.bfloat16)
            cols = slice(h * width, (h + 1) * width)
            within[low:high, cols] = jnp.dot(
                weights, values[:high, cols], preferred_element_type=jnp.float32
            ).astype(within.dtype)


def mix_kernel(blocks, count, lengths, states, mixed):
    def request(position):
        bound, found = 0, 0
        for k in range(lengths.shape[0]):
            bound = bound + lengths[k]
            found = found + jnp.where(position >= bound, 1, 0)
        return found

    begin = [request(b * count) for b in range(blocks)]
    end = [request((b + 1) * count - 1) for b in range(blocks)]
    total = jnp.zeros(states.shape[1:], jnp.float32)
    mixed[0] = total.astype(jnp.bfloat16)
    for b in range(1, blocks):
        whole = jnp.where(begin[b - 1] == end[b - 1], 1.0, 0.0)
        goes_on = jnp.where(end[b - 1] == begin[b], 1.0, 0.0)
        total = (states[b - 1].astype(jnp.float32) + whole * total) * goes_on
        mixed[b] = total.astype(jnp.bfloat16)


def finish_kernel(heads, width, info, lengths, within, query, carried, gains, first, second, scale,
                  normed):
    count = within.shape[0]
    rows = query[...]
    maps = []
    for h in range(heads):
        a = lax.dot_general(rows, table_of(first, h), NT, preferred_element_type=jnp.float32)
        b = lax.dot_general(rows, table_of(second, h), NT, preferred_element_type=jnp.float32)
        mapped = ((a + scale[0:1, :]) * (b + scale[1:2, :])) * scale[3:4, :]
        maps.append(mapped.astype(jnp.bfloat16))
    positions = lax.broadcasted_iota(jnp.int32, (count, 1), 0) + info[0] * count
    begin = request_of(jnp.zeros((1, 1), jnp.int32) + info[0] * count, lengths)
    follows = jnp.where(request_of(positions, lengths) == begin, 1.0, 0.0)
    for h in range(heads):
        cross = jnp.dot(maps[h], carried[h], preferred_element_type=jnp.float32)
        cols = slice(h * width, (h + 1) * width)
        combined = within[:, cols].astype(jnp.float32) + follows * cross
        factor = lax.rsqrt(jnp.mean(combined * combined, axis=-1, keepdims=True) + EPSILON)
        normed[:, cols] = (combined * factor * gains[:, cols]).astype(jnp.bfloat16)


def out_kernel(layout, tile, blocks, info, normed, *refs):
    pieces, (out,) = refs[: len(layout)], refs[len(layout) :]
    depth = normed.shape[1]
    step = depth // 4
    for near in range(blocks // 2):
        pair = (near, near + blocks // 2)
        total = None
        for row in range(0, depth, step):
            both = jnp.concatenate(
                [piece_rows(pieces, layout, slot, row, step) for slot in pair], axis=1
            )
            term = jnp.dot(normed[:, row : row + step], both, preferred_element_type=jnp.float32)
            total = term if total is None else total + term
        for k, slot in enumerate(pair):
            place = place_of(info[0], slot)
            at = jnp.where(place // (blocks // 2) == info[1], 0, blocks // 2) + place % (blocks // 2)
            out[at] = total[:, k * tile : (k + 1) * tile].astype(jnp.bfloat16)


def add_kernel(partial, received, out):
    tile = partial.shape[2]
    for k in range(received.shape[0]):
        total = partial[k].astype(jnp.float32) + received[k].astype(jnp.float32)
        out[:, k * tile : (k + 1) * tile] = total.astype(jnp.bfloat16)


def stay(array):
    return pltpu.with_memory_space_constraint(array, pltpu.HBM)


def call(kernel, name, mebibytes, cost, shapes, scalars, arrays, late=(), far=(), out_far=()):
    shapes = [jax.ShapeDtypeStruct(shape, kind) for shape, kind in shapes]
    n, m, k = len(scalars), len(arrays), len(shapes)
    held = [arrays[i] for i in far] + [shapes[i] for i in out_far]
    arrays = [stay(array) if i in far else array for i, array in enumerate(arrays)]
    shapes = [
        pltpu.HBM(shape.shape, shape.dtype) if i in out_far else shape
        for i, shape in enumerate(shapes)
    ]
    scratch = [pltpu.VMEM(array.shape, array.dtype) for array in held]
    if held:
        scratch.append(pltpu.SemaphoreType.DMA((len(held),)))

    def body(*refs):
        given, made = list(refs[: n + m]), list(refs[n + m + len(late) :])
        outs, buffers = made[:k], made[k:]
        copies = []
        for at, i in enumerate(far):
            copies.append(pltpu.make_async_copy(given[n + i], buffers[at], buffers[-1].at[at]))
            given[n + i] = buffers[at]
        for copy in copies:
            copy.start()
        for copy in copies:
            copy.wait()
        copies = []
        for at, i in enumerate(out_far, len(far)):
            copies.append(pltpu.make_async_copy(buffers[at], outs[i], buffers[-1].at[at]))
            outs[i] = buffers[at]
        kernel(*given, *outs)
        for copy in copies:
            copy.start()
        for copy in copies:
            copy.wait()

    return pl.pallas_call(
        body,
        out_shape=shapes,
        in_specs=[SMEM] * n
        + [HBM if i in far else VMEM for i in range(m)]
        + [ANY] * len(late),
        out_specs=[HBM if i in out_far else VMEM for i in range(k)],
        scratch_shapes=scratch,
        compiler_params=params(mebibytes),
        cost_estimate=pl.CostEstimate(flops=cost[0], bytes_accessed=cost[1], transcendentals=0),
        name=name,
    )(*scalars, *arrays, *late)


def per_device_fast(
    tokens,
    q_weight,
    k_weight,
    v_weight,
    adapter_down,
    adapter_up,
    lengths,
    adapter_ids,
    head_gain,
    out_weight,
):
    count, depth = tokens.shape
    blocks = lax.axis_size("dp")
    heads = q_weight.shape[1] // F
    width = v_weight.shape[1] // heads
    rows = v_weight.shape[0]
    wide, small, total = heads * width, heads * F, heads * (width + 2 * F)
    tile = out_weight.shape[1]
    half = jnp.bfloat16
    info = jnp.stack([lax.axis_index("dp"), lax.axis_index("mp")]).astype(jnp.int32)
    first, second, scale = feature_tables()

    alone, pair = join(v_weight, q_weight, k_weight)
    other = lax.ppermute(adapter_down, "mp", [(0, 1), (1, 0)])
    (turned,) = call(
        functools.partial(turn_kernel, rows), "turn", 8, (0, 4 * count * depth),
        [((count, depth), half)], [info], [tokens],
    )
    (low,) = call(
        low_kernel, "low", 8, (4 * count * depth * adapter_down.shape[1], 2 * count * depth),
        [((count, 2 * adapter_down.shape[1]), half)], [info, lengths, adapter_ids],
        [tokens, adapter_down, other],
    )

    chain = gather_rows(alone, pair)
    next(chain)
    second_round = chain.send(())
    third = next(chain)
    out_alone, out_pair = pack(
        [[(0, 0, wide // 2)], [(0, wide // 2, wide // 2)]], [out_weight], second_round[:2]
    )
    out_chain = gather_rows(out_alone, out_pair)
    out_first = next(out_chain)
    chain.send((turned, low) + out_first)
    out_second = out_chain.send(third[:2])
    fifth = chain.send(())
    gathered = next(chain)
    out_third = next(out_chain)

    pieces, layout = [piece for piece, _ in gathered], [places for _, places in gathered]
    query, keys, values, state = call(
        functools.partial(project_kernel, layout, rows, heads, width), "project", 14,
        (2 * count * depth * total, 2 * depth * total),
        [
            ((count, small), half),
            ((count, small), half),
            ((count, wide), half),
            ((heads, FEATS, width), half),
        ],
        [info, lengths], [turned, low, adapter_up, first, second, scale.T, *pieces], out_far=(0, 1, 2),
    )
    parts = state.reshape(blocks, heads * FEATS // blocks, width)
    parts = lax.all_to_all(parts, "dp", 0, 0, tiled=True)
    (within,) = call(
        functools.partial(within_kernel, heads, width), "within", 12,
        (4 * count * count * wide, 8 * count * wide), [((count, wide), half)],
        [info, lengths], [query, keys, values], far=(0, 1, 2),
    )
    out_fourth = out_chain.send(())
    out_chain.send(())
    out_gathered = next(out_chain)
    (mixed,) = call(
        functools.partial(mix_kernel, blocks, count), "mix", 4, (0, 4 * parts.size),
        [(parts.shape, half)], [lengths], [parts], (within,),
    )
    carried = lax.all_to_all(mixed, "dp", 0, 0, tiled=True).reshape(heads, FEATS, width)
    (normed,) = call(
        functools.partial(finish_kernel, heads, width), "finish", 10,
        (2 * count * FEATS * wide, 8 * count * wide), [((count, wide), half)],
        [info, lengths],
        [within, query, carried, head_gain.reshape(1, -1), first, second, scale], far=(1, 4, 5, 6),
    )
    pieces, layout = [piece for piece, _ in out_gathered], [places for _, places in out_gathered]
    (partial,) = call(
        functools.partial(out_kernel, layout, tile, blocks), "out", 12,
        (2 * count * wide * blocks * tile, 4 * count * blocks * tile),
        [((blocks, count, tile), half)], [info], [normed, *pieces],
    )
    received = lax.ppermute(partial[blocks // 2 :], "mp", [(0, 1), (1, 0)])
    (result,) = call(
        add_kernel, "add", 8, (0, 8 * count * wide), [((count, blocks // 2 * tile), half)], [],
        [partial, received],
    )
    return result


def solution(mesh):
    placed = (
        P("dp", None),
        P("dp", "mp"),
        P("dp", "mp"),
        P("dp", "mp"),
        P(None, "mp"),
        P(None, "mp"),
        P(),
        P(),
        P("mp"),
        P("mp", "dp"),
    )
    fast = mesh.shape["dp"] == 16 and mesh.shape["mp"] == 2
    return jax.shard_map(
        per_device_fast if fast else per_device_general,
        mesh=mesh,
        in_specs=placed,
        out_specs=P("dp", "mp"),
        check_vma=False,
    )
```

```python
import functools
import math

import jax
import jax.numpy as jnp
import numpy as np
from jax import lax
from jax.experimental import pallas as pl
from jax.experimental.pallas import tpu as pltpu
from jax.sharding import PartitionSpec as P

F = 16
R = 16
EPSILON = 1e-05
SQUARES = [(a, b) for a in range(F) for b in range(a, F)]
FEATS = 160
VMEM = pl.BlockSpec(memory_space=pltpu.VMEM)
SMEM = pl.BlockSpec(memory_space=pltpu.SMEM)
ANY = pl.BlockSpec(memory_space=pl.ANY)
HBM = pl.BlockSpec(memory_space=pltpu.HBM)


def carried_in(value, axis, combine, identity):
    length, place = (lax.axis_size(axis), lax.axis_index(axis))
    everything = jax.tree.map(
        lambda part, kind: lax.all_gather(part.astype(kind), axis),
        value,
        (jnp.bfloat16, jnp.bfloat16),
    )
    start = jax.tree.map(
        lambda part, zero: jnp.broadcast_to(jnp.asarray(zero, part.dtype), part.shape),
        value,
        identity,
    )

    def turn(k, before):
        reached = k < place
        new = combine(
            before, jax.tree.map(lambda part, own: part[k].astype(own.dtype), everything, value)
        )
        return jax.tree.map(lambda a, b: jnp.where(reached, a, b), new, before)

    return lax.fori_loop(0, length, turn, start)


def taylor(inputs):
    squares = (inputs[..., :, None] * inputs[..., None, :]).reshape(
        inputs.shape[:-1] + (inputs.shape[-1] * inputs.shape[-1],)
    )
    constant = jnp.ones(inputs.shape[:-1] + (1,), jnp.float32)
    return jnp.concatenate([constant, 0.5 * inputs, squares * (0.25 / math.sqrt(2.0))], axis=-1)


def token_tables(lengths, adapter_ids, positions):
    bounds = jnp.cumsum(lengths)
    request = jnp.sum((positions[:, None] >= bounds[None, :]).astype(jnp.int32), axis=1)
    openings = bounds - lengths
    starts = jnp.any(positions[:, None] == openings[None, :], axis=1)
    picked = request[:, None] == jnp.arange(lengths.shape[0], dtype=jnp.int32)[None, :]
    adapter = jnp.sum(jnp.where(picked, adapter_ids[None, :], 0), axis=1)
    return (request, starts, adapter)


def block_local(query, key_rows, values, request, starts):
    scores = jnp.einsum("ihd,jhd->hij", query, key_rows, preferred_element_type=jnp.float32) * 0.25
    weights = 1.0 + scores + 0.5 * scores * scores
    indexes = jnp.arange(request.shape[0], dtype=jnp.int32)
    allowed = (indexes[None, :] <= indexes[:, None]) & (request[None, :] == request[:, None])
    weights = jnp.where(allowed[None], weights, 0.0).astype(jnp.bfloat16)
    within = jnp.einsum("hij,jhe->ihe", weights, values, preferred_element_type=jnp.float32)
    query_map = taylor(query.astype(jnp.float32)).astype(jnp.bfloat16)
    key_map = taylor(key_rows.astype(jnp.float32)).astype(jnp.bfloat16)
    tail_mask = (request == request[-1]).astype(jnp.bfloat16)
    masked_keys = key_map * tail_mask[:, None, None]
    summary = jnp.einsum("ihf,ihe->hfe", masked_keys, values, preferred_element_type=jnp.float32)
    restart = jnp.max(starts.astype(jnp.float32))
    return (within, query_map, summary, restart)


def finish(within, query_map, carried, request, starts, gains):
    follows = ((request == request[0]) & jnp.logical_not(starts[0])).astype(jnp.float32)
    cross = jnp.einsum(
        "ihf,hfe->ihe", query_map, carried.astype(jnp.bfloat16), preferred_element_type=jnp.float32
    )
    combined = within + follows[:, None, None] * cross
    factor = lax.rsqrt(jnp.mean(combined * combined, axis=-1, keepdims=True) + EPSILON)
    return (combined * factor * gains[None]).astype(jnp.bfloat16)


def combine(earlier, later):
    return (
        jnp.maximum(earlier[0], later[0]),
        jnp.where(later[0] > 0, later[1], earlier[1] + later[1]),
    )


def per_device_general(
    tokens,
    q_weight,
    k_weight,
    v_weight,
    adapter_down,
    adapter_up,
    lengths,
    adapter_ids,
    head_gain,
    out_weight,
):
    row_count = tokens.shape[0]
    heads_here = q_weight.shape[1] // F
    value_width = v_weight.shape[1] // heads_here
    positions = lax.axis_index("dp") * row_count + jnp.arange(row_count, dtype=jnp.int32)
    request, starts, adapter = token_tables(lengths, adapter_ids, positions)
    together = lax.all_gather(
        jnp.concatenate([q_weight, k_weight, v_weight], axis=1), "dp", axis=0, tiled=True
    )
    sums = jnp.dot(tokens, together, preferred_element_type=jnp.float32)
    width = heads_here * F
    query = sums[:, :width].astype(jnp.bfloat16).reshape(row_count, heads_here, F)
    key_rows = sums[:, width : 2 * width].astype(jnp.bfloat16).reshape(row_count, heads_here, F)
    value_sum = sums[:, 2 * width :]
    piece = lax.all_gather(adapter_down, "mp", axis=1, tiled=True)
    partial_low = jnp.dot(tokens, piece, preferred_element_type=jnp.float32)
    owners = jnp.arange(piece.shape[1], dtype=jnp.int32) // R
    low_rank = jnp.where(adapter[:, None] == owners[None, :], partial_low, 0.0).astype(jnp.bfloat16)
    values = value_sum + jnp.dot(low_rank, adapter_up, preferred_element_type=jnp.float32)
    values = values.astype(jnp.bfloat16).reshape(row_count, heads_here, value_width)
    within, query_map, summary, restart = block_local(query, key_rows, values, request, starts)
    identity = (jnp.zeros((), jnp.float32), jnp.zeros_like(summary))
    _, carried = carried_in((restart, summary), "dp", combine, identity)
    gains = head_gain.reshape(heads_here, value_width)
    normed = finish(within, query_map, carried, request, starts, gains).reshape(
        row_count, heads_here * value_width
    )
    partial_terms = jnp.dot(
        normed,
        lax.all_gather(out_weight, "dp", axis=1, tiled=True),
        preferred_element_type=jnp.float32,
    )
    return lax.psum_scatter(
        partial_terms.astype(jnp.bfloat16), "mp", scatter_dimension=1, tiled=True
    )


def feature_tables():
    first = np.zeros((FEATS, 128), np.float32)
    second = np.zeros((FEATS, 128), np.float32)
    scale = np.zeros((8, FEATS), np.float32)
    scale[:, 0] = 1.0
    for a in range(F):
        first[1 + a, a] = 1.0
        scale[1, 1 + a] = 1.0
        scale[2, 1 + a] = scale[3, 1 + a] = 0.5
    for at, (a, b) in enumerate(SQUARES):
        row = 1 + F + at
        first[row, a] = second[row, b] = 1.0
        scale[2, row] = 0.25 / math.sqrt(2.0)
        scale[3, row] = (0.25 if a == b else 0.5) / math.sqrt(2.0)
    return jnp.asarray(first), jnp.asarray(second), jnp.asarray(scale)


def table_of(table, head):
    turned = pltpu.roll(table[...], head * F, 1) if head else table[...]
    return turned.astype(jnp.bfloat16)


def chip(place, x):
    z, y = (place, 0) if place < 4 else (7 - place, 1)
    return z * 4 + y * 2 + x


def moves(step, flip):
    return [
        (chip(r, x), chip((r + step) % 8, x ^ flip)) for r in range(8) for x in range(2)
    ]


UP, DOWN, ACROSS = moves(1, 0), moves(-1, 0), moves(0, 1)


def place_of(here, slot):
    z, y, x = here // 4, (here // 2) % 2, here % 2
    there = (jnp.where(y == 0, z, 7 - z) + slot % 8) % 8
    base = jnp.where(there < 4, there * 4, (7 - there) * 4 + 2)
    return base + (x if slot < 8 else 1 - x)


def request_of(positions, lengths):
    bound, request = 0, jnp.zeros_like(positions)
    for k in range(lengths.shape[0]):
        bound = bound + lengths[k]
        request = request + jnp.where(positions >= bound, 1, 0)
    return request


def params(mebibytes):
    return pltpu.CompilerParams(vmem_limit_bytes=mebibytes * 1024 * 1024)


def send(value, pairs):
    return lax.ppermute(value, "dp", pairs)


def pack_kernel(recipes, sources, *refs):
    for recipe, out in zip(recipes, refs[len(refs) - len(recipes) :]):
        row = 0
        for source, start, rows in recipe:
            out[row : row + rows, :] = refs[source][start : start + rows, :]
            row += rows


def pack(recipes, sources, late=()):
    wide = sources[0].shape[1]
    return pl.pallas_call(
        functools.partial(pack_kernel, recipes, len(sources)),
        out_shape=[
            jax.ShapeDtypeStruct((sum(part[2] for part in recipe), wide), jnp.bfloat16)
            for recipe in recipes
        ],
        in_specs=[VMEM] * len(sources) + [ANY] * len(late),
        out_specs=[VMEM] * len(recipes),
        compiler_params=params(6),
        name="pack",
    )(*sources, *late)


def gather_rows(alone, pair):
    h = alone.shape[0]
    n, q = 2 * h, h // 2
    up1, down1, across = send(alone, UP), send(alone, DOWN), send(pair, ACROSS)
    late = yield up1, down1, across
    to_up, to_down, to_x = pack(
        [
            [(1, 0, h), (2, 0, h), (3, 0, h)],
            [(1, 0, h), (2, 0, h), (4, 0, h)],
            [(0, 0, h), (3, 0, h), (4, 0, h)],
        ],
        [alone, pair, across, up1, down1],
        late,
    )
    up2, down2, x1 = send(to_up, UP), send(to_down, DOWN), send(to_x, ACROSS)
    yield up2, down2, x1
    up3, down3 = send(up2, UP), send(down2, DOWN)
    (to_x,) = pack([[(0, n, h), (1, n, h)]], [up2, down2])
    x2 = send(to_x, ACROSS)
    late = yield up3, down3, x2
    to_up, to_down, to_x = pack(
        [[(0, 0, n + q)], [(1, 0, n), (1, n + q, q)], [(0, n, h), (1, n, h)]],
        [up3, down3],
        (x1,) + tuple(late),
    )
    up4, down4, x3 = send(to_up, UP), send(to_down, DOWN), send(to_x, ACROSS)
    late = yield up4, down4, x3
    to_up, to_down, to_x = pack(
        [[(0, 0, h)], [(1, h, h)], [(0, n, q), (1, n, q)]], [up4, down4], (x2,) + tuple(late)
    )
    up5, down5, x4 = send(to_up, UP), send(to_down, DOWN), send(to_x, ACROSS)
    yield up5, down5, x4
    yield [
        (alone, [(0, 0, h, 0)]),
        (pair, [(0, h, h, 0)]),
        (across, [(8, h, h, 0)]),
        (up1, [(7, 0, h, 0)]),
        (down1, [(1, 0, h, 0)]),
        (x1, [(8, 0, h, 0), (15, 0, h, h), (9, 0, h, n)]),
        (up2, [(7, h, h, 0), (15, h, h, h), (6, 0, h, n)]),
        (down2, [(1, h, h, 0), (9, h, h, h), (2, 0, h, n)]),
        (x2, [(14, 0, h, 0), (10, 0, h, h)]),
        (up3, [(6, h, h, 0), (14, h, h, h), (5, 0, h, n)]),
        (down3, [(2, h, h, 0), (10, h, h, h), (3, 0, h, n)]),
        (x3, [(13, 0, h, 0), (11, 0, h, h)]),
        (up4, [(5, h, h, 0), (13, h, h, h), (4, 0, q, n)]),
        (down4, [(3, h, h, 0), (11, h, h, h), (4, q, q, n)]),
        (x4, [(12, 0, h, 0)]),
        (up5, [(4, h, h, 0)]),
        (down5, [(12, h, h, 0)]),
    ]


def piece_rows(pieces, layout, slot, row, rows, cols=slice(None)):
    found = []
    while rows:
        for piece, places in zip(pieces, layout):
            for at, first, count, source in places:
                if at == slot and first <= row < first + count and rows:
                    take = min(rows, first + count - row)
                    start = source + row - first
                    found.append(piece[start : start + take, cols])
                    row, rows = row + take, rows - take
    return found[0] if len(found) == 1 else jnp.concatenate(found, axis=0)


NT = (((1,), (1,)), ((), ()))


def join_kernel(values, query, keys, alone, pair, done):
    half, wide = alone.shape[0], values.shape[1]
    small = query.shape[1]
    copies = []
    for out, row in ((alone, 0), (pair, half)):
        for source, at in ((values, 0), (query, wide), (keys, wide + small)):
            copies.append(
                pltpu.make_async_copy(
                    source.at[pl.ds(row, half)],
                    out.at[:, pl.ds(at, source.shape[1])],
                    done.at[len(copies)],
                )
            )
    for copy in copies:
        copy.start()
    for copy in copies:
        copy.wait()


def join(values, query, keys):
    rows, wide = values.shape[0], values.shape[1] + query.shape[1] + keys.shape[1]
    return pl.pallas_call(
        join_kernel,
        out_shape=[jax.ShapeDtypeStruct((rows // 2, wide), values.dtype)] * 2,
        in_specs=[HBM] * 3,
        out_specs=[VMEM] * 2,
        scratch_shapes=[pltpu.SemaphoreType.DMA((6,))],
        compiler_params=params(4),
        name="join",
    )(stay(values), stay(query), stay(keys))


def turn_kernel(rows, info, tokens, turned):
    for slot in range(tokens.shape[1] // rows):
        source = pl.ds(pl.multiple_of(place_of(info[0], slot) * rows, rows), rows)
        turned[:, slot * rows : (slot + 1) * rows] = tokens[:, source]


def low_kernel(info, lengths, adapter_ids, tokens, own, other, low):
    count, wide = tokens.shape[0], own.shape[1]
    positions = lax.broadcasted_iota(jnp.int32, (count, 1), 0) + info[0] * count
    request = request_of(positions, lengths)
    adapter = jnp.zeros_like(request)
    for k in range(lengths.shape[0]):
        adapter = jnp.where(request == k, adapter_ids[k], adapter)
    owners = lax.broadcasted_iota(jnp.int32, (1, wide), 1) // R
    for piece, place in ((own, info[1]), (other, 1 - info[1])):
        partial = jnp.dot(tokens[...], piece[...], preferred_element_type=jnp.float32)
        kept = adapter == owners + place * (wide // R)
        cols = pl.ds(pl.multiple_of(place * wide, wide), wide)
        low[:, cols] = jnp.where(kept, partial, 0.0).astype(jnp.bfloat16)


def project_kernel(layout, rows, heads, width, info, lengths, tokens, low, up, first, second,
                   scale, *refs):
    pieces, (query, keys, values, state) = refs[: len(layout)], refs[len(layout) :]
    count, depth = tokens.shape
    wide = heads * width
    small = heads * F

    def product(cols):
        total = None
        for slot in range(0, depth // rows, 2):
            weight = jnp.concatenate(
                [piece_rows(pieces, layout, at, 0, rows, cols) for at in (slot, slot + 1)], axis=0
            )
            term = jnp.dot(
                tokens[:, slot * rows : (slot + 2) * rows], weight,
                preferred_element_type=jnp.float32,
            )
            total = term if total is None else total + term
        return total

    both = product(slice(wide, wide + 2 * small))
    query[...] = both[:, :small].astype(jnp.bfloat16)
    key_rows = both[:, small:].astype(jnp.bfloat16)
    keys[...] = key_rows
    positions = lax.broadcasted_iota(jnp.int32, (1, count), 1) + info[0] * count
    end = request_of(jnp.full((1, 1), count - 1, jnp.int32) + info[0] * count, lengths)
    tail = jnp.where(request_of(positions, lengths) == end, 1.0, 0.0)
    maps = []
    for h in range(heads):
        a = lax.dot_general(table_of(first, h), key_rows, NT, preferred_element_type=jnp.float32)
        b = lax.dot_general(table_of(second, h), key_rows, NT, preferred_element_type=jnp.float32)
        mapped = ((a + scale[:, 0:1]) * (b + scale[:, 1:2])) * scale[:, 2:3]
        maps.append((mapped * tail).astype(jnp.bfloat16))
    for h in range(0, heads, 2):
        cols = slice(h * width, (h + 2) * width)
        total = product(cols)
        total += jnp.dot(low[...], up[:, cols], preferred_element_type=jnp.float32)
        values[:, cols] = total.astype(jnp.bfloat16)
    for h in range(heads):
        state[h] = jnp.dot(
            maps[h], values[:, h * width : (h + 1) * width], preferred_element_type=jnp.float32
        ).astype(jnp.bfloat16)


def within_kernel(heads, width, info, lengths, query, keys, values, within):
    count = query.shape[0]
    cut = count // 2
    lanes = lax.broadcasted_iota(jnp.int32, (1, heads * F), 1)
    start = info[0] * count
    row = request_of(lax.broadcasted_iota(jnp.int32, (1, count), 1) + start, lengths)
    col = request_of(lax.broadcasted_iota(jnp.int32, (count, 1), 0) + start, lengths)
    for low, high in ((0, cut), (cut, count)):
        i = lax.broadcasted_iota(jnp.int32, (high - low, high), 0) + low
        j = lax.broadcasted_iota(jnp.int32, (high - low, high), 1)
        allowed = (j <= i) & (row[:, :high] == col[low:high, :])
        for h in range(heads):
            mine = jnp.where(lanes // F == h, 0.25, 0.0).astype(jnp.bfloat16)
            s = lax.dot_general(
                query[low:high, :] * mine, keys[:high, :], NT, preferred_element_type=jnp.float32
            )
            weights = 1.0 + s + 0.5 * s * s
            weights = jnp.where(allowed, weights, 0.0).astype(jnp.bfloat16)
            cols = slice(h * width, (h + 1) * width)
            within[low:high, cols] = jnp.dot(
                weights, values[:high, cols], preferred_element_type=jnp.float32
            ).astype(within.dtype)


def mix_kernel(blocks, count, lengths, states, mixed):
    def request(position):
        bound, found = 0, 0
        for k in range(lengths.shape[0]):
            bound = bound + lengths[k]
            found = found + jnp.where(position >= bound, 1, 0)
        return found

    begin = [request(b * count) for b in range(blocks)]
    end = [request((b + 1) * count - 1) for b in range(blocks)]
    total = jnp.zeros(states.shape[1:], jnp.float32)
    mixed[0] = total.astype(jnp.bfloat16)
    for b in range(1, blocks):
        whole = jnp.where(begin[b - 1] == end[b - 1], 1.0, 0.0)
        goes_on = jnp.where(end[b - 1] == begin[b], 1.0, 0.0)
        total = (states[b - 1].astype(jnp.float32) + whole * total) * goes_on
        mixed[b] = total.astype(jnp.bfloat16)


def finish_kernel(heads, width, info, lengths, within, query, carried, gains, first, second, scale,
                  normed):
    count = within.shape[0]
    rows = query[...]
    maps = []
    for h in range(heads):
        a = lax.dot_general(rows, table_of(first, h), NT, preferred_element_type=jnp.float32)
        b = lax.dot_general(rows, table_of(second, h), NT, preferred_element_type=jnp.float32)
        mapped = ((a + scale[0:1, :]) * (b + scale[1:2, :])) * scale[3:4, :]
        maps.append(mapped.astype(jnp.bfloat16))
    positions = lax.broadcasted_iota(jnp.int32, (count, 1), 0) + info[0] * count
    begin = request_of(jnp.zeros((1, 1), jnp.int32) + info[0] * count, lengths)
    follows = jnp.where(request_of(positions, lengths) == begin, 1.0, 0.0)
    for h in range(heads):
        cross = jnp.dot(maps[h], carried[h], preferred_element_type=jnp.float32)
        cols = slice(h * width, (h + 1) * width)
        combined = within[:, cols].astype(jnp.float32) + follows * cross
        factor = lax.rsqrt(jnp.mean(combined * combined, axis=-1, keepdims=True) + EPSILON)
        normed[:, cols] = (combined * factor * gains[:, cols]).astype(jnp.bfloat16)


def out_kernel(layout, tile, blocks, info, normed, *refs):
    pieces, (out,) = refs[: len(layout)], refs[len(layout) :]
    depth = normed.shape[1]
    step = depth // 4
    for near in range(blocks // 2):
        pair = (near, near + blocks // 2)
        total = None
        for row in range(0, depth, step):
            both = jnp.concatenate(
                [piece_rows(pieces, layout, slot, row, step) for slot in pair], axis=1
            )
            term = jnp.dot(normed[:, row : row + step], both, preferred_element_type=jnp.float32)
            total = term if total is None else total + term
        for k, slot in enumerate(pair):
            place = place_of(info[0], slot)
            at = jnp.where(place // (blocks // 2) == info[1], 0, blocks // 2) + place % (blocks // 2)
            out[at] = total[:, k * tile : (k + 1) * tile].astype(jnp.bfloat16)


def add_kernel(partial, received, out):
    tile = partial.shape[2]
    for k in range(received.shape[0]):
        total = partial[k].astype(jnp.float32) + received[k].astype(jnp.float32)
        out[:, k * tile : (k + 1) * tile] = total.astype(jnp.bfloat16)


def stay(array):
    return pltpu.with_memory_space_constraint(array, pltpu.HBM)


def call(kernel, name, mebibytes, cost, shapes, scalars, arrays, late=(), far=(), out_far=()):
    shapes = [jax.ShapeDtypeStruct(shape, kind) for shape, kind in shapes]
    n, m, k = len(scalars), len(arrays), len(shapes)
    held = [arrays[i] for i in far] + [shapes[i] for i in out_far]
    arrays = [stay(array) if i in far else array for i, array in enumerate(arrays)]
    shapes = [
        pltpu.HBM(shape.shape, shape.dtype) if i in out_far else shape
        for i, shape in enumerate(shapes)
    ]
    scratch = [pltpu.VMEM(array.shape, array.dtype) for array in held]
    if held:
        scratch.append(pltpu.SemaphoreType.DMA((len(held),)))

    def body(*refs):
        given, made = list(refs[: n + m]), list(refs[n + m + len(late) :])
        outs, buffers = made[:k], made[k:]
        copies = []
        for at, i in enumerate(far):
            copies.append(pltpu.make_async_copy(given[n + i], buffers[at], buffers[-1].at[at]))
            given[n + i] = buffers[at]
        for copy in copies:
            copy.start()
        for copy in copies:
            copy.wait()
        copies = []
        for at, i in enumerate(out_far, len(far)):
            copies.append(pltpu.make_async_copy(buffers[at], outs[i], buffers[-1].at[at]))
            outs[i] = buffers[at]
        kernel(*given, *outs)
        for copy in copies:
            copy.start()
        for copy in copies:
            copy.wait()

    return pl.pallas_call(
        body,
        out_shape=shapes,
        in_specs=[SMEM] * n
        + [HBM if i in far else VMEM for i in range(m)]
        + [ANY] * len(late),
        out_specs=[HBM if i in out_far else VMEM for i in range(k)],
        scratch_shapes=scratch,
        compiler_params=params(mebibytes),
        cost_estimate=pl.CostEstimate(flops=cost[0], bytes_accessed=cost[1], transcendentals=0),
        name=name,
    )(*scalars, *arrays, *late)


def per_device_fast(
    tokens,
    q_weight,
    k_weight,
    v_weight,
    adapter_down,
    adapter_up,
    lengths,
    adapter_ids,
    head_gain,
    out_weight,
):
    count, depth = tokens.shape
    blocks = lax.axis_size("dp")
    heads = q_weight.shape[1] // F
    width = v_weight.shape[1] // heads
    rows = v_weight.shape[0]
    wide, small, total = heads * width, heads * F, heads * (width + 2 * F)
    tile = out_weight.shape[1]
    half = jnp.bfloat16
    info = jnp.stack([lax.axis_index("dp"), lax.axis_index("mp")]).astype(jnp.int32)
    first, second, scale = feature_tables()

    alone, pair = join(v_weight, q_weight, k_weight)
    other = lax.ppermute(adapter_down, "mp", [(0, 1), (1, 0)])
    (turned,) = call(
        functools.partial(turn_kernel, rows), "turn", 8, (0, 4 * count * depth),
        [((count, depth), half)], [info], [tokens],
    )
    (low,) = call(
        low_kernel, "low", 8, (4 * count * depth * adapter_down.shape[1], 2 * count * depth),
        [((count, 2 * adapter_down.shape[1]), half)], [info, lengths, adapter_ids],
        [tokens, adapter_down, other],
    )

    chain = gather_rows(alone, pair)
    next(chain)
    second_round = chain.send(())
    third = next(chain)
    out_alone, out_pair = pack(
        [[(0, 0, wide // 2)], [(0, wide // 2, wide // 2)]], [out_weight], second_round[:2] + (turned, low)
    )
    out_chain = gather_rows(out_alone, out_pair)
    out_first = next(out_chain)
    chain.send(out_first)
    out_second = out_chain.send(third[:2])
    fifth = chain.send(())
    gathered = next(chain)
    out_third = next(out_chain)

    pieces, layout = [piece for piece, _ in gathered], [places for _, places in gathered]
    query, keys, values, state = call(
        functools.partial(project_kernel, layout, rows, heads, width), "project", 14,
        (count * depth * total // 2, depth * total // 2),
        [
            ((count, small), half),
            ((count, small), half),
            ((count, wide), half),
            ((heads, FEATS, width), half),
        ],
        [info, lengths], [turned, low, adapter_up, first, second, scale.T, *pieces], out_far=(0, 1, 2),
    )
    parts = state.reshape(blocks, heads * FEATS // blocks, width)
    parts = lax.all_to_all(parts, "dp", 0, 0, tiled=True)
    (within,) = call(
        functools.partial(within_kernel, heads, width), "within", 12,
        (12 * count * count * wide, 24 * count * wide), [((count, wide), half)],
        [info, lengths], [query, keys, values], far=(0, 1, 2),
    )
    out_fourth = out_chain.send(())
    out_chain.send(())
    out_gathered = next(out_chain)
    (mixed,) = call(
        functools.partial(mix_kernel, blocks, count), "mix", 4, (0, 4 * parts.size),
        [(parts.shape, half)], [lengths], [parts], (within,),
    )
    carried = lax.all_to_all(mixed, "dp", 0, 0, tiled=True).reshape(heads, FEATS, width)
    (normed,) = call(
        functools.partial(finish_kernel, heads, width), "finish", 10,
        (2 * count * FEATS * wide, 8 * count * wide), [((count, wide), half)],
        [info, lengths],
        [within, query, carried, head_gain.reshape(1, -1), first, second, scale], far=(1, 4, 5, 6),
    )
    pieces, layout = [piece for piece, _ in out_gathered], [places for _, places in out_gathered]
    (partial,) = call(
        functools.partial(out_kernel, layout, tile, blocks), "out", 12,
        (2 * count * wide * blocks * tile, 4 * count * blocks * tile),
        [((blocks, count, tile), half)], [info], [normed, *pieces],
    )
    received = lax.ppermute(partial[blocks // 2 :], "mp", [(0, 1), (1, 0)])
    (result,) = call(
        add_kernel, "add", 8, (0, 8 * count * wide), [((count, blocks // 2 * tile), half)], [],
        [partial, received],
    )
    return result


def solution(mesh):
    placed = (
        P("dp", None),
        P("dp", "mp"),
        P("dp", "mp"),
        P("dp", "mp"),
        P(None, "mp"),
        P(None, "mp"),
        P(),
        P(),
        P("mp"),
        P("mp", "dp"),
    )
    fast = mesh.shape["dp"] == 16 and mesh.shape["mp"] == 2
    return jax.shard_map(
        per_device_fast if fast else per_device_general,
        mesh=mesh,
        in_specs=placed,
        out_specs=P("dp", "mp"),
        check_vma=False,
    )
```

```python
import functools
import math

import jax
import jax.numpy as jnp
import numpy as np
from jax import lax
from jax.experimental import pallas as pl
from jax.experimental.pallas import tpu as pltpu
from jax.sharding import PartitionSpec as P

F = 16
R = 16
EPSILON = 1e-05
SQUARES = [(a, b) for a in range(F) for b in range(a, F)]
FEATS = 160
VMEM = pl.BlockSpec(memory_space=pltpu.VMEM)
SMEM = pl.BlockSpec(memory_space=pltpu.SMEM)
ANY = pl.BlockSpec(memory_space=pl.ANY)
HBM = pl.BlockSpec(memory_space=pltpu.HBM)


def carried_in(value, axis, combine, identity):
    length, place = (lax.axis_size(axis), lax.axis_index(axis))
    everything = jax.tree.map(
        lambda part, kind: lax.all_gather(part.astype(kind), axis),
        value,
        (jnp.bfloat16, jnp.bfloat16),
    )
    start = jax.tree.map(
        lambda part, zero: jnp.broadcast_to(jnp.asarray(zero, part.dtype), part.shape),
        value,
        identity,
    )

    def turn(k, before):
        reached = k < place
        new = combine(
            before, jax.tree.map(lambda part, own: part[k].astype(own.dtype), everything, value)
        )
        return jax.tree.map(lambda a, b: jnp.where(reached, a, b), new, before)

    return lax.fori_loop(0, length, turn, start)


def taylor(inputs):
    squares = (inputs[..., :, None] * inputs[..., None, :]).reshape(
        inputs.shape[:-1] + (inputs.shape[-1] * inputs.shape[-1],)
    )
    constant = jnp.ones(inputs.shape[:-1] + (1,), jnp.float32)
    return jnp.concatenate([constant, 0.5 * inputs, squares * (0.25 / math.sqrt(2.0))], axis=-1)


def token_tables(lengths, adapter_ids, positions):
    bounds = jnp.cumsum(lengths)
    request = jnp.sum((positions[:, None] >= bounds[None, :]).astype(jnp.int32), axis=1)
    openings = bounds - lengths
    starts = jnp.any(positions[:, None] == openings[None, :], axis=1)
    picked = request[:, None] == jnp.arange(lengths.shape[0], dtype=jnp.int32)[None, :]
    adapter = jnp.sum(jnp.where(picked, adapter_ids[None, :], 0), axis=1)
    return (request, starts, adapter)


def block_local(query, key_rows, values, request, starts):
    scores = jnp.einsum("ihd,jhd->hij", query, key_rows, preferred_element_type=jnp.float32) * 0.25
    weights = 1.0 + scores + 0.5 * scores * scores
    indexes = jnp.arange(request.shape[0], dtype=jnp.int32)
    allowed = (indexes[None, :] <= indexes[:, None]) & (request[None, :] == request[:, None])
    weights = jnp.where(allowed[None], weights, 0.0).astype(jnp.bfloat16)
    within = jnp.einsum("hij,jhe->ihe", weights, values, preferred_element_type=jnp.float32)
    query_map = taylor(query.astype(jnp.float32)).astype(jnp.bfloat16)
    key_map = taylor(key_rows.astype(jnp.float32)).astype(jnp.bfloat16)
    tail_mask = (request == request[-1]).astype(jnp.bfloat16)
    masked_keys = key_map * tail_mask[:, None, None]
    summary = jnp.einsum("ihf,ihe->hfe", masked_keys, values, preferred_element_type=jnp.float32)
    restart = jnp.max(starts.astype(jnp.float32))
    return (within, query_map, summary, restart)


def finish(within, query_map, carried, request, starts, gains):
    follows = ((request == request[0]) & jnp.logical_not(starts[0])).astype(jnp.float32)
    cross = jnp.einsum(
        "ihf,hfe->ihe", query_map, carried.astype(jnp.bfloat16), preferred_element_type=jnp.float32
    )
    combined = within + follows[:, None, None] * cross
    factor = lax.rsqrt(jnp.mean(combined * combined, axis=-1, keepdims=True) + EPSILON)
    return (combined * factor * gains[None]).astype(jnp.bfloat16)


def combine(earlier, later):
    return (
        jnp.maximum(earlier[0], later[0]),
        jnp.where(later[0] > 0, later[1], earlier[1] + later[1]),
    )


def per_device_general(
    tokens,
    q_weight,
    k_weight,
    v_weight,
    adapter_down,
    adapter_up,
    lengths,
    adapter_ids,
    head_gain,
    out_weight,
):
    row_count = tokens.shape[0]
    heads_here = q_weight.shape[1] // F
    value_width = v_weight.shape[1] // heads_here
    positions = lax.axis_index("dp") * row_count + jnp.arange(row_count, dtype=jnp.int32)
    request, starts, adapter = token_tables(lengths, adapter_ids, positions)
    together = lax.all_gather(
        jnp.concatenate([q_weight, k_weight, v_weight], axis=1), "dp", axis=0, tiled=True
    )
    sums = jnp.dot(tokens, together, preferred_element_type=jnp.float32)
    width = heads_here * F
    query = sums[:, :width].astype(jnp.bfloat16).reshape(row_count, heads_here, F)
    key_rows = sums[:, width : 2 * width].astype(jnp.bfloat16).reshape(row_count, heads_here, F)
    value_sum = sums[:, 2 * width :]
    piece = lax.all_gather(adapter_down, "mp", axis=1, tiled=True)
    partial_low = jnp.dot(tokens, piece, preferred_element_type=jnp.float32)
    owners = jnp.arange(piece.shape[1], dtype=jnp.int32) // R
    low_rank = jnp.where(adapter[:, None] == owners[None, :], partial_low, 0.0).astype(jnp.bfloat16)
    values = value_sum + jnp.dot(low_rank, adapter_up, preferred_element_type=jnp.float32)
    values = values.astype(jnp.bfloat16).reshape(row_count, heads_here, value_width)
    within, query_map, summary, restart = block_local(query, key_rows, values, request, starts)
    identity = (jnp.zeros((), jnp.float32), jnp.zeros_like(summary))
    _, carried = carried_in((restart, summary), "dp", combine, identity)
    gains = head_gain.reshape(heads_here, value_width)
    normed = finish(within, query_map, carried, request, starts, gains).reshape(
        row_count, heads_here * value_width
    )
    partial_terms = jnp.dot(
        normed,
        lax.all_gather(out_weight, "dp", axis=1, tiled=True),
        preferred_element_type=jnp.float32,
    )
    return lax.psum_scatter(
        partial_terms.astype(jnp.bfloat16), "mp", scatter_dimension=1, tiled=True
    )


def feature_tables():
    first = np.zeros((FEATS, 128), np.float32)
    second = np.zeros((FEATS, 128), np.float32)
    scale = np.zeros((8, FEATS), np.float32)
    scale[:, 0] = 1.0
    for a in range(F):
        first[1 + a, a] = 1.0
        scale[1, 1 + a] = 1.0
        scale[2, 1 + a] = scale[3, 1 + a] = 0.5
    for at, (a, b) in enumerate(SQUARES):
        row = 1 + F + at
        first[row, a] = second[row, b] = 1.0
        scale[2, row] = 0.25 / math.sqrt(2.0)
        scale[3, row] = (0.25 if a == b else 0.5) / math.sqrt(2.0)
    return jnp.asarray(first), jnp.asarray(second), jnp.asarray(scale)


def table_of(table, head):
    turned = pltpu.roll(table[...], head * F, 1) if head else table[...]
    return turned.astype(jnp.bfloat16)


def chip(place, x):
    z, y = (place, 0) if place < 4 else (7 - place, 1)
    return z * 4 + y * 2 + x


def moves(step, flip):
    return [
        (chip(r, x), chip((r + step) % 8, x ^ flip)) for r in range(8) for x in range(2)
    ]


UP, DOWN, ACROSS = moves(1, 0), moves(-1, 0), moves(0, 1)


def place_of(here, slot):
    z, y, x = here // 4, (here // 2) % 2, here % 2
    there = (jnp.where(y == 0, z, 7 - z) + slot % 8) % 8
    base = jnp.where(there < 4, there * 4, (7 - there) * 4 + 2)
    return base + (x if slot < 8 else 1 - x)


def request_of(positions, lengths):
    bound, request = 0, jnp.zeros_like(positions)
    for k in range(lengths.shape[0]):
        bound = bound + lengths[k]
        request = request + jnp.where(positions >= bound, 1, 0)
    return request


def params(mebibytes):
    return pltpu.CompilerParams(vmem_limit_bytes=mebibytes * 1024 * 1024)


def send(value, pairs):
    return lax.ppermute(value, "dp", pairs)


def pack_kernel(recipes, sources, *refs):
    for recipe, out in zip(recipes, refs[len(refs) - len(recipes) :]):
        row = 0
        for source, start, rows in recipe:
            out[row : row + rows, :] = refs[source][start : start + rows, :]
            row += rows


def pack(recipes, sources, late=()):
    wide = sources[0].shape[1]
    return pl.pallas_call(
        functools.partial(pack_kernel, recipes, len(sources)),
        out_shape=[
            jax.ShapeDtypeStruct((sum(part[2] for part in recipe), wide), jnp.bfloat16)
            for recipe in recipes
        ],
        in_specs=[VMEM] * len(sources) + [ANY] * len(late),
        out_specs=[VMEM] * len(recipes),
        compiler_params=params(6),
        name="pack",
    )(*sources, *late)


def gather_rows(alone, pair):
    h = alone.shape[0]
    n, q = 2 * h, h // 2
    up1, down1, across = send(alone, UP), send(alone, DOWN), send(pair, ACROSS)
    late = yield up1, down1, across
    to_up, to_down, to_x = pack(
        [
            [(1, 0, h), (2, 0, h), (3, 0, h)],
            [(1, 0, h), (2, 0, h), (4, 0, h)],
            [(0, 0, h), (3, 0, h), (4, 0, h)],
        ],
        [alone, pair, across, up1, down1],
        late,
    )
    up2, down2, x1 = send(to_up, UP), send(to_down, DOWN), send(to_x, ACROSS)
    yield up2, down2, x1
    up3, down3 = send(up2, UP), send(down2, DOWN)
    (to_x,) = pack([[(0, n, h), (1, n, h)]], [up2, down2])
    x2 = send(to_x, ACROSS)
    late = yield up3, down3, x2
    to_up, to_down, to_x = pack(
        [[(0, 0, n + q)], [(1, 0, n), (1, n + q, q)], [(0, n, h), (1, n, h)]],
        [up3, down3],
        (x1,) + tuple(late),
    )
    up4, down4, x3 = send(to_up, UP), send(to_down, DOWN), send(to_x, ACROSS)
    late = yield up4, down4, x3
    to_up, to_down, to_x = pack(
        [[(0, 0, h)], [(1, h, h)], [(0, n, q), (1, n, q)]], [up4, down4], (x2,) + tuple(late)
    )
    up5, down5, x4 = send(to_up, UP), send(to_down, DOWN), send(to_x, ACROSS)
    yield up5, down5, x4
    yield [
        (alone, [(0, 0, h, 0)]),
        (pair, [(0, h, h, 0)]),
        (across, [(8, h, h, 0)]),
        (up1, [(7, 0, h, 0)]),
        (down1, [(1, 0, h, 0)]),
        (x1, [(8, 0, h, 0), (15, 0, h, h), (9, 0, h, n)]),
        (up2, [(7, h, h, 0), (15, h, h, h), (6, 0, h, n)]),
        (down2, [(1, h, h, 0), (9, h, h, h), (2, 0, h, n)]),
        (x2, [(14, 0, h, 0), (10, 0, h, h)]),
        (up3, [(6, h, h, 0), (14, h, h, h), (5, 0, h, n)]),
        (down3, [(2, h, h, 0), (10, h, h, h), (3, 0, h, n)]),
        (x3, [(13, 0, h, 0), (11, 0, h, h)]),
        (up4, [(5, h, h, 0), (13, h, h, h), (4, 0, q, n)]),
        (down4, [(3, h, h, 0), (11, h, h, h), (4, q, q, n)]),
        (x4, [(12, 0, h, 0)]),
        (up5, [(4, h, h, 0)]),
        (down5, [(12, h, h, 0)]),
    ]


def piece_rows(pieces, layout, slot, row, rows, cols=slice(None)):
    found = []
    while rows:
        for piece, places in zip(pieces, layout):
            for at, first, count, source in places:
                if at == slot and first <= row < first + count and rows:
                    take = min(rows, first + count - row)
                    start = source + row - first
                    found.append(piece[start : start + take, cols])
                    row, rows = row + take, rows - take
    return found[0] if len(found) == 1 else jnp.concatenate(found, axis=0)


NT = (((1,), (1,)), ((), ()))


def join_kernel(values, query, keys, alone, pair, done):
    half, wide = alone.shape[0], values.shape[1]
    small = query.shape[1]
    copies = []
    for out, row in ((alone, 0), (pair, half)):
        for source, at in ((values, 0), (query, wide), (keys, wide + small)):
            copies.append(
                pltpu.make_async_copy(
                    source.at[pl.ds(row, half)],
                    out.at[:, pl.ds(at, source.shape[1])],
                    done.at[len(copies)],
                )
            )
    for copy in copies:
        copy.start()
    for copy in copies:
        copy.wait()


def join(values, query, keys):
    rows, wide = values.shape[0], values.shape[1] + query.shape[1] + keys.shape[1]
    return pl.pallas_call(
        join_kernel,
        out_shape=[jax.ShapeDtypeStruct((rows // 2, wide), values.dtype)] * 2,
        in_specs=[HBM] * 3,
        out_specs=[VMEM] * 2,
        scratch_shapes=[pltpu.SemaphoreType.DMA((6,))],
        compiler_params=params(4),
        name="join",
    )(stay(values), stay(query), stay(keys))


def turn_kernel(rows, info, tokens, turned):
    for slot in range(tokens.shape[1] // rows):
        source = pl.ds(pl.multiple_of(place_of(info[0], slot) * rows, rows), rows)
        turned[:, slot * rows : (slot + 1) * rows] = tokens[:, source]


def low_kernel(info, lengths, adapter_ids, tokens, own, other, low):
    count, wide = tokens.shape[0], own.shape[1]
    positions = lax.broadcasted_iota(jnp.int32, (count, 1), 0) + info[0] * count
    request = request_of(positions, lengths)
    adapter = jnp.zeros_like(request)
    for k in range(lengths.shape[0]):
        adapter = jnp.where(request == k, adapter_ids[k], adapter)
    owners = lax.broadcasted_iota(jnp.int32, (1, wide), 1) // R
    for piece, place in ((own, info[1]), (other, 1 - info[1])):
        partial = jnp.dot(tokens[...], piece[...], preferred_element_type=jnp.float32)
        kept = adapter == owners + place * (wide // R)
        cols = pl.ds(pl.multiple_of(place * wide, wide), wide)
        low[:, cols] = jnp.where(kept, partial, 0.0).astype(jnp.bfloat16)


def project_kernel(layout, rows, heads, width, info, lengths, tokens, low, up, first, second,
                   scale, *refs):
    pieces, (query, keys, values, state) = refs[: len(layout)], refs[len(layout) :]
    count, depth = tokens.shape
    wide = heads * width
    small = heads * F

    def product(cols):
        total = None
        for slot in range(0, depth // rows, 2):
            weight = jnp.concatenate(
                [piece_rows(pieces, layout, at, 0, rows, cols) for at in (slot, slot + 1)], axis=0
            )
            term = jnp.dot(
                tokens[:, slot * rows : (slot + 2) * rows], weight,
                preferred_element_type=jnp.float32,
            )
            total = term if total is None else total + term
        return total

    both = product(slice(wide, wide + 2 * small))
    query[...] = both[:, :small].astype(jnp.bfloat16)
    key_rows = both[:, small:].astype(jnp.bfloat16)
    keys[...] = key_rows
    positions = lax.broadcasted_iota(jnp.int32, (1, count), 1) + info[0] * count
    end = request_of(jnp.full((1, 1), count - 1, jnp.int32) + info[0] * count, lengths)
    tail = jnp.where(request_of(positions, lengths) == end, 1.0, 0.0)
    maps = []
    for h in range(heads):
        a = lax.dot_general(table_of(first, h), key_rows, NT, preferred_element_type=jnp.float32)
        b = lax.dot_general(table_of(second, h), key_rows, NT, preferred_element_type=jnp.float32)
        mapped = ((a + scale[:, 0:1]) * (b + scale[:, 1:2])) * scale[:, 2:3]
        maps.append((mapped * tail).astype(jnp.bfloat16))
    for h in range(0, heads, 2):
        cols = slice(h * width, (h + 2) * width)
        total = product(cols)
        total += jnp.dot(low[...], up[:, cols], preferred_element_type=jnp.float32)
        values[:, cols] = total.astype(jnp.bfloat16)
    for h in range(heads):
        state[h] = jnp.dot(
            maps[h], values[:, h * width : (h + 1) * width], preferred_element_type=jnp.float32
        ).astype(jnp.bfloat16)


def within_kernel(heads, width, info, lengths, query, keys, values, within):
    count = query.shape[0]
    cut = count // 2
    lanes = lax.broadcasted_iota(jnp.int32, (1, heads * F), 1)
    start = info[0] * count
    row = request_of(lax.broadcasted_iota(jnp.int32, (1, count), 1) + start, lengths)
    col = request_of(lax.broadcasted_iota(jnp.int32, (count, 1), 0) + start, lengths)
    for low, high in ((0, cut), (cut, count)):
        i = lax.broadcasted_iota(jnp.int32, (high - low, high), 0) + low
        j = lax.broadcasted_iota(jnp.int32, (high - low, high), 1)
        allowed = (j <= i) & (row[:, :high] == col[low:high, :])
        for h in range(heads):
            mine = jnp.where(lanes // F == h, 0.25, 0.0).astype(jnp.bfloat16)
            s = lax.dot_general(
                query[low:high, :] * mine, keys[:high, :], NT, preferred_element_type=jnp.float32
            )
            weights = 1.0 + s + 0.5 * s * s
            weights = jnp.where(allowed, weights, 0.0).astype(jnp.bfloat16)
            cols = slice(h * width, (h + 1) * width)
            within[low:high, cols] = jnp.dot(
                weights, values[:high, cols], preferred_element_type=jnp.float32
            ).astype(within.dtype)


def mix_kernel(blocks, count, lengths, states, mixed):
    def request(position):
        bound, found = 0, 0
        for k in range(lengths.shape[0]):
            bound = bound + lengths[k]
            found = found + jnp.where(position >= bound, 1, 0)
        return found

    begin = [request(b * count) for b in range(blocks)]
    end = [request((b + 1) * count - 1) for b in range(blocks)]
    total = jnp.zeros(states.shape[1:], jnp.float32)
    mixed[0] = total.astype(jnp.bfloat16)
    for b in range(1, blocks):
        whole = jnp.where(begin[b - 1] == end[b - 1], 1.0, 0.0)
        goes_on = jnp.where(end[b - 1] == begin[b], 1.0, 0.0)
        total = (states[b - 1].astype(jnp.float32) + whole * total) * goes_on
        mixed[b] = total.astype(jnp.bfloat16)


def finish_kernel(heads, width, info, lengths, within, query, carried, gains, first, second, scale,
                  normed):
    count = within.shape[0]
    rows = query[...]
    maps = []
    for h in range(heads):
        a = lax.dot_general(rows, table_of(first, h), NT, preferred_element_type=jnp.float32)
        b = lax.dot_general(rows, table_of(second, h), NT, preferred_element_type=jnp.float32)
        mapped = ((a + scale[0:1, :]) * (b + scale[1:2, :])) * scale[3:4, :]
        maps.append(mapped.astype(jnp.bfloat16))
    positions = lax.broadcasted_iota(jnp.int32, (count, 1), 0) + info[0] * count
    begin = request_of(jnp.zeros((1, 1), jnp.int32) + info[0] * count, lengths)
    follows = jnp.where(request_of(positions, lengths) == begin, 1.0, 0.0)
    for h in range(heads):
        cross = jnp.dot(maps[h], carried[h], preferred_element_type=jnp.float32)
        cols = slice(h * width, (h + 1) * width)
        combined = within[:, cols].astype(jnp.float32) + follows * cross
        factor = lax.rsqrt(jnp.mean(combined * combined, axis=-1, keepdims=True) + EPSILON)
        normed[:, cols] = (combined * factor * gains[:, cols]).astype(jnp.bfloat16)


def out_block(layout, tile, blocks, info, normed, pieces, near):
    depth = normed.shape[1]
    step = depth // 4
    pair = (near, near + blocks // 2)
    total = None
    for row in range(0, depth, step):
        both = jnp.concatenate(
            [piece_rows(pieces, layout, slot, row, step) for slot in pair], axis=1
        )
        term = jnp.dot(normed[:, row : row + step], both, preferred_element_type=jnp.float32)
        total = term if total is None else total + term
    found = []
    for k, slot in enumerate(pair):
        place = place_of(info[0], slot)
        at = jnp.where(place // (blocks // 2) == info[1], 0, blocks // 2) + place % (blocks // 2)
        found.append((at, total[:, k * tile : (k + 1) * tile].astype(jnp.bfloat16)))
    return found


def out_kernel(layout, tile, blocks, info, normed, *refs):
    pieces, (out,) = refs[: len(layout)], refs[len(layout) :]
    for near in range(blocks // 2):
        if near != blocks // 4:
            for at, part in out_block(layout, tile, blocks, info, normed, pieces, near):
                out[at] = part


def last_kernel(layout, tile, blocks, info, normed, *refs):
    pieces, (_, out, held, done) = refs[: len(layout)], refs[len(layout) :]
    copies = []
    for at, part in out_block(layout, tile, blocks, info, normed, pieces, blocks // 4):
        k = len(copies)
        held[k] = part
        copies.append(pltpu.make_async_copy(held.at[k], out.at[at], done.at[k]))
        copies[-1].start()
    for copy in copies:
        copy.wait()


def add_kernel(partial, received, out):
    tile = partial.shape[2]
    for k in range(received.shape[0]):
        total = partial[k].astype(jnp.float32) + received[k].astype(jnp.float32)
        out[:, k * tile : (k + 1) * tile] = total.astype(jnp.bfloat16)


def stay(array):
    return pltpu.with_memory_space_constraint(array, pltpu.HBM)


def call(kernel, name, mebibytes, cost, shapes, scalars, arrays, late=(), far=(), out_far=()):
    shapes = [jax.ShapeDtypeStruct(shape, kind) for shape, kind in shapes]
    n, m, k = len(scalars), len(arrays), len(shapes)
    held = [arrays[i] for i in far] + [shapes[i] for i in out_far]
    arrays = [stay(array) if i in far else array for i, array in enumerate(arrays)]
    shapes = [
        pltpu.HBM(shape.shape, shape.dtype) if i in out_far else shape
        for i, shape in enumerate(shapes)
    ]
    scratch = [pltpu.VMEM(array.shape, array.dtype) for array in held]
    if held:
        scratch.append(pltpu.SemaphoreType.DMA((len(held),)))

    def body(*refs):
        given, made = list(refs[: n + m]), list(refs[n + m + len(late) :])
        outs, buffers = made[:k], made[k:]
        copies = []
        for at, i in enumerate(far):
            copies.append(pltpu.make_async_copy(given[n + i], buffers[at], buffers[-1].at[at]))
            given[n + i] = buffers[at]
        for copy in copies:
            copy.start()
        for copy in copies:
            copy.wait()
        copies = []
        for at, i in enumerate(out_far, len(far)):
            copies.append(pltpu.make_async_copy(buffers[at], outs[i], buffers[-1].at[at]))
            outs[i] = buffers[at]
        kernel(*given, *outs)
        for copy in copies:
            copy.start()
        for copy in copies:
            copy.wait()

    return pl.pallas_call(
        body,
        out_shape=shapes,
        in_specs=[SMEM] * n
        + [HBM if i in far else VMEM for i in range(m)]
        + [ANY] * len(late),
        out_specs=[HBM if i in out_far else VMEM for i in range(k)],
        scratch_shapes=scratch,
        compiler_params=params(mebibytes),
        cost_estimate=pl.CostEstimate(flops=cost[0], bytes_accessed=cost[1], transcendentals=0),
        name=name,
    )(*scalars, *arrays, *late)


def per_device_fast(
    tokens,
    q_weight,
    k_weight,
    v_weight,
    adapter_down,
    adapter_up,
    lengths,
    adapter_ids,
    head_gain,
    out_weight,
):
    count, depth = tokens.shape
    blocks = lax.axis_size("dp")
    heads = q_weight.shape[1] // F
    width = v_weight.shape[1] // heads
    rows = v_weight.shape[0]
    wide, small, total = heads * width, heads * F, heads * (width + 2 * F)
    tile = out_weight.shape[1]
    half = jnp.bfloat16
    info = jnp.stack([lax.axis_index("dp"), lax.axis_index("mp")]).astype(jnp.int32)
    first, second, scale = feature_tables()

    alone, pair = join(v_weight, q_weight, k_weight)
    other = lax.ppermute(adapter_down, "mp", [(0, 1), (1, 0)])
    (turned,) = call(
        functools.partial(turn_kernel, rows), "turn", 8, (0, 4 * count * depth),
        [((count, depth), half)], [info], [tokens],
    )
    (low,) = call(
        low_kernel, "low", 8, (4 * count * depth * adapter_down.shape[1], 2 * count * depth),
        [((count, 2 * adapter_down.shape[1]), half)], [info, lengths, adapter_ids],
        [tokens, adapter_down, other],
    )

    chain = gather_rows(alone, pair)
    next(chain)
    second_round = chain.send(())
    third = next(chain)
    out_alone, out_pair = pack(
        [[(0, 0, wide // 2)], [(0, wide // 2, wide // 2)]], [out_weight], second_round[:2] + (turned, low)
    )
    out_chain = gather_rows(out_alone, out_pair)
    out_first = next(out_chain)
    chain.send(out_first)
    out_second = out_chain.send(third[:2])
    fifth = chain.send(())
    gathered = next(chain)
    out_third = next(out_chain)

    pieces, layout = [piece for piece, _ in gathered], [places for _, places in gathered]
    query, keys, values, state = call(
        functools.partial(project_kernel, layout, rows, heads, width), "project", 14,
        (count * depth * total // 2, depth * total // 2),
        [
            ((count, small), half),
            ((count, small), half),
            ((count, wide), half),
            ((heads, FEATS, width), half),
        ],
        [info, lengths], [turned, low, adapter_up, first, second, scale.T, *pieces], out_far=(0, 1, 2),
    )
    parts = state.reshape(blocks, heads * FEATS // blocks, width)
    parts = lax.all_to_all(parts, "dp", 0, 0, tiled=True)
    (within,) = call(
        functools.partial(within_kernel, heads, width), "within", 12,
        (12 * count * count * wide, 24 * count * wide), [((count, wide), half)],
        [info, lengths], [query, keys, values], far=(0, 1, 2),
    )
    out_fourth = out_chain.send(())
    (mixed,) = call(
        functools.partial(mix_kernel, blocks, count), "mix", 4, (0, 4 * parts.size),
        [(parts.shape, half)], [lengths], [parts], (within,),
    )
    carried = lax.all_to_all(mixed, "dp", 0, 0, tiled=True).reshape(heads, FEATS, width)
    (normed,) = call(
        functools.partial(finish_kernel, heads, width), "finish", 10,
        (2 * count * FEATS * wide, 8 * count * wide), [((count, wide), half)],
        [info, lengths],
        [within, query, carried, head_gain.reshape(1, -1), first, second, scale], far=(1, 4, 5, 6),
    )
    out_chain.send((normed,))
    out_gathered = next(out_chain)
    far_slots = (blocks // 4, 3 * blocks // 4)
    early = [(p, l) for p, l in out_gathered if not all(place[0] in far_slots for place in l)]
    last = [(p, l) for p, l in out_gathered if any(place[0] in far_slots for place in l)]
    (partial,) = call(
        functools.partial(out_kernel, [l for _, l in early], tile, blocks), "out", 12,
        (2 * count * wide * blocks * tile, 4 * count * blocks * tile),
        [((blocks, count, tile), half)], [info], [normed] + [p for p, _ in early],
    )
    partial = pl.pallas_call(
        functools.partial(last_kernel, [l for _, l in last], tile, blocks),
        out_shape=jax.ShapeDtypeStruct(partial.shape, partial.dtype),
        in_specs=[SMEM] + [VMEM] * (1 + len(last)) + [ANY],
        out_specs=ANY,
        scratch_shapes=[
            pltpu.VMEM((2, count, tile), half),
            pltpu.SemaphoreType.DMA((2,)),
        ],
        input_output_aliases={2 + len(last): 0},
        compiler_params=params(8),
        name="last",
    )(info, normed, *[p for p, _ in last], partial)
    received = lax.ppermute(partial[blocks // 2 :], "mp", [(0, 1), (1, 0)])
    (result,) = call(
        add_kernel, "add", 8, (0, 8 * count * wide), [((count, blocks // 2 * tile), half)], [],
        [partial, received],
    )
    return result


def solution(mesh):
    placed = (
        P("dp", None),
        P("dp", "mp"),
        P("dp", "mp"),
        P("dp", "mp"),
        P(None, "mp"),
        P(None, "mp"),
        P(),
        P(),
        P("mp"),
        P("mp", "dp"),
    )
    fast = mesh.shape["dp"] == 16 and mesh.shape["mp"] == 2
    return jax.shard_map(
        per_device_fast if fast else per_device_general,
        mesh=mesh,
        in_specs=placed,
        out_specs=P("dp", "mp"),
        check_vma=False,
    )
```

```python
import functools
import math

import jax
import jax.numpy as jnp
import numpy as np
from jax import lax
from jax.experimental import pallas as pl
from jax.experimental.pallas import tpu as pltpu
from jax.sharding import PartitionSpec as P

F = 16
R = 16
EPSILON = 1e-05
SQUARES = [(a, b) for a in range(F) for b in range(a, F)]
FEATS = 160
VMEM = pl.BlockSpec(memory_space=pltpu.VMEM)
SMEM = pl.BlockSpec(memory_space=pltpu.SMEM)
ANY = pl.BlockSpec(memory_space=pl.ANY)
HBM = pl.BlockSpec(memory_space=pltpu.HBM)


def carried_in(value, axis, combine, identity):
    length, place = (lax.axis_size(axis), lax.axis_index(axis))
    everything = jax.tree.map(
        lambda part, kind: lax.all_gather(part.astype(kind), axis),
        value,
        (jnp.bfloat16, jnp.bfloat16),
    )
    start = jax.tree.map(
        lambda part, zero: jnp.broadcast_to(jnp.asarray(zero, part.dtype), part.shape),
        value,
        identity,
    )

    def turn(k, before):
        reached = k < place
        new = combine(
            before, jax.tree.map(lambda part, own: part[k].astype(own.dtype), everything, value)
        )
        return jax.tree.map(lambda a, b: jnp.where(reached, a, b), new, before)

    return lax.fori_loop(0, length, turn, start)


def taylor(inputs):
    squares = (inputs[..., :, None] * inputs[..., None, :]).reshape(
        inputs.shape[:-1] + (inputs.shape[-1] * inputs.shape[-1],)
    )
    constant = jnp.ones(inputs.shape[:-1] + (1,), jnp.float32)
    return jnp.concatenate([constant, 0.5 * inputs, squares * (0.25 / math.sqrt(2.0))], axis=-1)


def token_tables(lengths, adapter_ids, positions):
    bounds = jnp.cumsum(lengths)
    request = jnp.sum((positions[:, None] >= bounds[None, :]).astype(jnp.int32), axis=1)
    openings = bounds - lengths
    starts = jnp.any(positions[:, None] == openings[None, :], axis=1)
    picked = request[:, None] == jnp.arange(lengths.shape[0], dtype=jnp.int32)[None, :]
    adapter = jnp.sum(jnp.where(picked, adapter_ids[None, :], 0), axis=1)
    return (request, starts, adapter)


def block_local(query, key_rows, values, request, starts):
    scores = jnp.einsum("ihd,jhd->hij", query, key_rows, preferred_element_type=jnp.float32) * 0.25
    weights = 1.0 + scores + 0.5 * scores * scores
    indexes = jnp.arange(request.shape[0], dtype=jnp.int32)
    allowed = (indexes[None, :] <= indexes[:, None]) & (request[None, :] == request[:, None])
    weights = jnp.where(allowed[None], weights, 0.0).astype(jnp.bfloat16)
    within = jnp.einsum("hij,jhe->ihe", weights, values, preferred_element_type=jnp.float32)
    query_map = taylor(query.astype(jnp.float32)).astype(jnp.bfloat16)
    key_map = taylor(key_rows.astype(jnp.float32)).astype(jnp.bfloat16)
    tail_mask = (request == request[-1]).astype(jnp.bfloat16)
    masked_keys = key_map * tail_mask[:, None, None]
    summary = jnp.einsum("ihf,ihe->hfe", masked_keys, values, preferred_element_type=jnp.float32)
    restart = jnp.max(starts.astype(jnp.float32))
    return (within, query_map, summary, restart)


def finish(within, query_map, carried, request, starts, gains):
    follows = ((request == request[0]) & jnp.logical_not(starts[0])).astype(jnp.float32)
    cross = jnp.einsum(
        "ihf,hfe->ihe", query_map, carried.astype(jnp.bfloat16), preferred_element_type=jnp.float32
    )
    combined = within + follows[:, None, None] * cross
    factor = lax.rsqrt(jnp.mean(combined * combined, axis=-1, keepdims=True) + EPSILON)
    return (combined * factor * gains[None]).astype(jnp.bfloat16)


def combine(earlier, later):
    return (
        jnp.maximum(earlier[0], later[0]),
        jnp.where(later[0] > 0, later[1], earlier[1] + later[1]),
    )


def per_device_general(
    tokens,
    q_weight,
    k_weight,
    v_weight,
    adapter_down,
    adapter_up,
    lengths,
    adapter_ids,
    head_gain,
    out_weight,
):
    row_count = tokens.shape[0]
    heads_here = q_weight.shape[1] // F
    value_width = v_weight.shape[1] // heads_here
    positions = lax.axis_index("dp") * row_count + jnp.arange(row_count, dtype=jnp.int32)
    request, starts, adapter = token_tables(lengths, adapter_ids, positions)
    together = lax.all_gather(
        jnp.concatenate([q_weight, k_weight, v_weight], axis=1), "dp", axis=0, tiled=True
    )
    sums = jnp.dot(tokens, together, preferred_element_type=jnp.float32)
    width = heads_here * F
    query = sums[:, :width].astype(jnp.bfloat16).reshape(row_count, heads_here, F)
    key_rows = sums[:, width : 2 * width].astype(jnp.bfloat16).reshape(row_count, heads_here, F)
    value_sum = sums[:, 2 * width :]
    piece = lax.all_gather(adapter_down, "mp", axis=1, tiled=True)
    partial_low = jnp.dot(tokens, piece, preferred_element_type=jnp.float32)
    owners = jnp.arange(piece.shape[1], dtype=jnp.int32) // R
    low_rank = jnp.where(adapter[:, None] == owners[None, :], partial_low, 0.0).astype(jnp.bfloat16)
    values = value_sum + jnp.dot(low_rank, adapter_up, preferred_element_type=jnp.float32)
    values = values.astype(jnp.bfloat16).reshape(row_count, heads_here, value_width)
    within, query_map, summary, restart = block_local(query, key_rows, values, request, starts)
    identity = (jnp.zeros((), jnp.float32), jnp.zeros_like(summary))
    _, carried = carried_in((restart, summary), "dp", combine, identity)
    gains = head_gain.reshape(heads_here, value_width)
    normed = finish(within, query_map, carried, request, starts, gains).reshape(
        row_count, heads_here * value_width
    )
    partial_terms = jnp.dot(
        normed,
        lax.all_gather(out_weight, "dp", axis=1, tiled=True),
        preferred_element_type=jnp.float32,
    )
    return lax.psum_scatter(
        partial_terms.astype(jnp.bfloat16), "mp", scatter_dimension=1, tiled=True
    )


def feature_tables():
    first = np.zeros((FEATS, 128), np.float32)
    second = np.zeros((FEATS, 128), np.float32)
    scale = np.zeros((8, FEATS), np.float32)
    scale[:, 0] = 1.0
    for a in range(F):
        first[1 + a, a] = 1.0
        scale[1, 1 + a] = 1.0
        scale[2, 1 + a] = scale[3, 1 + a] = 0.5
    for at, (a, b) in enumerate(SQUARES):
        row = 1 + F + at
        first[row, a] = second[row, b] = 1.0
        scale[2, row] = 0.25 / math.sqrt(2.0)
        scale[3, row] = (0.25 if a == b else 0.5) / math.sqrt(2.0)
    return jnp.asarray(first), jnp.asarray(second), jnp.asarray(scale)


def table_of(table, head):
    turned = pltpu.roll(table[...], head * F, 1) if head else table[...]
    return turned.astype(jnp.bfloat16)


def chip(place, x):
    z, y = (place, 0) if place < 4 else (7 - place, 1)
    return z * 4 + y * 2 + x


def moves(step, flip):
    return [
        (chip(r, x), chip((r + step) % 8, x ^ flip)) for r in range(8) for x in range(2)
    ]


UP, DOWN, ACROSS = moves(1, 0), moves(-1, 0), moves(0, 1)


def place_of(here, slot):
    z, y, x = here // 4, (here // 2) % 2, here % 2
    there = (jnp.where(y == 0, z, 7 - z) + slot % 8) % 8
    base = jnp.where(there < 4, there * 4, (7 - there) * 4 + 2)
    return base + (x if slot < 8 else 1 - x)


def request_of(positions, lengths):
    bound, request = 0, jnp.zeros_like(positions)
    for k in range(lengths.shape[0]):
        bound = bound + lengths[k]
        request = request + jnp.where(positions >= bound, 1, 0)
    return request


def params(mebibytes):
    return pltpu.CompilerParams(vmem_limit_bytes=mebibytes * 1024 * 1024)


def send(value, pairs):
    return lax.ppermute(value, "dp", pairs)


def pack_kernel(recipes, sources, *refs):
    for recipe, out in zip(recipes, refs[len(refs) - len(recipes) :]):
        row = 0
        for source, start, rows in recipe:
            out[row : row + rows, :] = refs[source][start : start + rows, :]
            row += rows


def pack(recipes, sources, late=()):
    wide = sources[0].shape[1]
    return pl.pallas_call(
        functools.partial(pack_kernel, recipes, len(sources)),
        out_shape=[
            jax.ShapeDtypeStruct((sum(part[2] for part in recipe), wide), jnp.bfloat16)
            for recipe in recipes
        ],
        in_specs=[VMEM] * len(sources) + [ANY] * len(late),
        out_specs=[VMEM] * len(recipes),
        compiler_params=params(6),
        name="pack",
    )(*sources, *late)


def gather_rows(alone, pair):
    h = alone.shape[0]
    n, q = 2 * h, h // 2
    up1, down1, across = send(alone, UP), send(alone, DOWN), send(pair, ACROSS)
    late = yield up1, down1, across
    to_up, to_down, to_x = pack(
        [
            [(1, 0, h), (2, 0, h), (3, 0, h)],
            [(1, 0, h), (2, 0, h), (4, 0, h)],
            [(0, 0, h), (3, 0, h), (4, 0, h)],
        ],
        [alone, pair, across, up1, down1],
        late,
    )
    up2, down2, x1 = send(to_up, UP), send(to_down, DOWN), send(to_x, ACROSS)
    yield up2, down2, x1
    up3, down3 = send(up2, UP), send(down2, DOWN)
    (to_x,) = pack([[(0, n, h), (1, n, h)]], [up2, down2])
    x2 = send(to_x, ACROSS)
    late = yield up3, down3, x2
    to_up, to_down, to_x = pack(
        [[(0, 0, n + q)], [(1, 0, n), (1, n + q, q)], [(0, n, h), (1, n, h)]],
        [up3, down3],
        (x1,) + tuple(late),
    )
    up4, down4, x3 = send(to_up, UP), send(to_down, DOWN), send(to_x, ACROSS)
    late = yield up4, down4, x3
    to_up, to_down, to_x = pack(
        [[(0, 0, h)], [(1, h, h)], [(0, n, q), (1, n, q)]], [up4, down4], (x2,) + tuple(late)
    )
    up5, down5, x4 = send(to_up, UP), send(to_down, DOWN), send(to_x, ACROSS)
    yield up5, down5, x4
    yield [
        (alone, [(0, 0, h, 0)]),
        (pair, [(0, h, h, 0)]),
        (across, [(8, h, h, 0)]),
        (up1, [(7, 0, h, 0)]),
        (down1, [(1, 0, h, 0)]),
        (x1, [(8, 0, h, 0), (15, 0, h, h), (9, 0, h, n)]),
        (up2, [(7, h, h, 0), (15, h, h, h), (6, 0, h, n)]),
        (down2, [(1, h, h, 0), (9, h, h, h), (2, 0, h, n)]),
        (x2, [(14, 0, h, 0), (10, 0, h, h)]),
        (up3, [(6, h, h, 0), (14, h, h, h), (5, 0, h, n)]),
        (down3, [(2, h, h, 0), (10, h, h, h), (3, 0, h, n)]),
        (x3, [(13, 0, h, 0), (11, 0, h, h)]),
        (up4, [(5, h, h, 0), (13, h, h, h), (4, 0, q, n)]),
        (down4, [(3, h, h, 0), (11, h, h, h), (4, q, q, n)]),
        (x4, [(12, 0, h, 0)]),
        (up5, [(4, h, h, 0)]),
        (down5, [(12, h, h, 0)]),
    ]


def piece_rows(pieces, layout, slot, row, rows, cols=slice(None)):
    found = []
    while rows:
        for piece, places in zip(pieces, layout):
            for at, first, count, source in places:
                if at == slot and first <= row < first + count and rows:
                    take = min(rows, first + count - row)
                    start = source + row - first
                    found.append(piece[start : start + take, cols])
                    row, rows = row + take, rows - take
    return found[0] if len(found) == 1 else jnp.concatenate(found, axis=0)


NT = (((1,), (1,)), ((), ()))


def join_kernel(values, query, keys, alone, pair, done):
    half, wide = alone.shape[0], values.shape[1]
    small = query.shape[1]
    copies = []
    for out, row in ((alone, 0), (pair, half)):
        for source, at in ((values, 0), (query, wide), (keys, wide + small)):
            copies.append(
                pltpu.make_async_copy(
                    source.at[pl.ds(row, half)],
                    out.at[:, pl.ds(at, source.shape[1])],
                    done.at[len(copies)],
                )
            )
    for copy in copies:
        copy.start()
    for copy in copies:
        copy.wait()


def join(values, query, keys):
    rows, wide = values.shape[0], values.shape[1] + query.shape[1] + keys.shape[1]
    return pl.pallas_call(
        join_kernel,
        out_shape=[jax.ShapeDtypeStruct((rows // 2, wide), values.dtype)] * 2,
        in_specs=[HBM] * 3,
        out_specs=[VMEM] * 2,
        scratch_shapes=[pltpu.SemaphoreType.DMA((6,))],
        compiler_params=params(4),
        name="join",
    )(stay(values), stay(query), stay(keys))


def turn_kernel(rows, info, tokens, turned):
    for slot in range(tokens.shape[1] // rows):
        source = pl.ds(pl.multiple_of(place_of(info[0], slot) * rows, rows), rows)
        turned[:, slot * rows : (slot + 1) * rows] = tokens[:, source]


def low_kernel(info, lengths, adapter_ids, tokens, own, other, low):
    count, wide = tokens.shape[0], own.shape[1]
    positions = lax.broadcasted_iota(jnp.int32, (count, 1), 0) + info[0] * count
    request = request_of(positions, lengths)
    adapter = jnp.zeros_like(request)
    for k in range(lengths.shape[0]):
        adapter = jnp.where(request == k, adapter_ids[k], adapter)
    owners = lax.broadcasted_iota(jnp.int32, (1, wide), 1) // R
    for piece, place in ((own, info[1]), (other, 1 - info[1])):
        partial = jnp.dot(tokens[...], piece[...], preferred_element_type=jnp.float32)
        kept = adapter == owners + place * (wide // R)
        cols = pl.ds(pl.multiple_of(place * wide, wide), wide)
        low[:, cols] = jnp.where(kept, partial, 0.0).astype(jnp.bfloat16)


def project_kernel(layout, rows, heads, width, info, lengths, tokens, low, up, first, second,
                   scale, *refs, flush):
    pieces, (query, keys, values, state) = refs[: len(layout)], refs[len(layout) :]
    count, depth = tokens.shape
    wide = heads * width
    small = heads * F

    def product(cols):
        total = None
        for slot in range(0, depth // rows, 2):
            weight = jnp.concatenate(
                [piece_rows(pieces, layout, at, 0, rows, cols) for at in (slot, slot + 1)], axis=0
            )
            term = jnp.dot(
                tokens[:, slot * rows : (slot + 2) * rows], weight,
                preferred_element_type=jnp.float32,
            )
            total = term if total is None else total + term
        return total

    both = product(slice(wide, wide + 2 * small))
    query[...] = both[:, :small].astype(jnp.bfloat16)
    key_rows = both[:, small:].astype(jnp.bfloat16)
    keys[...] = key_rows
    flush[0]()
    flush[1]()
    positions = lax.broadcasted_iota(jnp.int32, (1, count), 1) + info[0] * count
    end = request_of(jnp.full((1, 1), count - 1, jnp.int32) + info[0] * count, lengths)
    tail = jnp.where(request_of(positions, lengths) == end, 1.0, 0.0)
    maps = []
    for h in range(heads):
        a = lax.dot_general(table_of(first, h), key_rows, NT, preferred_element_type=jnp.float32)
        b = lax.dot_general(table_of(second, h), key_rows, NT, preferred_element_type=jnp.float32)
        mapped = ((a + scale[:, 0:1]) * (b + scale[:, 1:2])) * scale[:, 2:3]
        maps.append((mapped * tail).astype(jnp.bfloat16))
    for h in range(0, heads, 2):
        cols = slice(h * width, (h + 2) * width)
        total = product(cols)
        total += jnp.dot(low[...], up[:, cols], preferred_element_type=jnp.float32)
        values[:, cols] = total.astype(jnp.bfloat16)
    flush[2]()
    for h in range(heads):
        state[h] = jnp.dot(
            maps[h], values[:, h * width : (h + 1) * width], preferred_element_type=jnp.float32
        ).astype(jnp.bfloat16)


def within_kernel(heads, width, info, lengths, query, keys, values, within):
    count = query.shape[0]
    cut = count // 2
    lanes = lax.broadcasted_iota(jnp.int32, (1, heads * F), 1)
    start = info[0] * count
    row = request_of(lax.broadcasted_iota(jnp.int32, (1, count), 1) + start, lengths)
    col = request_of(lax.broadcasted_iota(jnp.int32, (count, 1), 0) + start, lengths)
    for low, high in ((0, cut), (cut, count)):
        i = lax.broadcasted_iota(jnp.int32, (high - low, high), 0) + low
        j = lax.broadcasted_iota(jnp.int32, (high - low, high), 1)
        allowed = (j <= i) & (row[:, :high] == col[low:high, :])
        for h in range(heads):
            mine = jnp.where(lanes // F == h, 0.25, 0.0).astype(jnp.bfloat16)
            s = lax.dot_general(
                query[low:high, :] * mine, keys[:high, :], NT, preferred_element_type=jnp.float32
            )
            weights = 1.0 + s + 0.5 * s * s
            weights = jnp.where(allowed, weights, 0.0).astype(jnp.bfloat16)
            cols = slice(h * width, (h + 1) * width)
            within[low:high, cols] = jnp.dot(
                weights, values[:high, cols], preferred_element_type=jnp.float32
            ).astype(within.dtype)


def mix_kernel(blocks, count, lengths, states, mixed):
    def request(position):
        bound, found = 0, 0
        for k in range(lengths.shape[0]):
            bound = bound + lengths[k]
            found = found + jnp.where(position >= bound, 1, 0)
        return found

    begin = [request(b * count) for b in range(blocks)]
    end = [request((b + 1) * count - 1) for b in range(blocks)]
    total = jnp.zeros(states.shape[1:], jnp.float32)
    mixed[0] = total.astype(jnp.bfloat16)
    for b in range(1, blocks):
        whole = jnp.where(begin[b - 1] == end[b - 1], 1.0, 0.0)
        goes_on = jnp.where(end[b - 1] == begin[b], 1.0, 0.0)
        total = (states[b - 1].astype(jnp.float32) + whole * total) * goes_on
        mixed[b] = total.astype(jnp.bfloat16)


def finish_kernel(heads, width, info, lengths, within, query, carried, gains, first, second, scale,
                  normed):
    count = within.shape[0]
    rows = query[...]
    maps = []
    for h in range(heads):
        a = lax.dot_general(rows, table_of(first, h), NT, preferred_element_type=jnp.float32)
        b = lax.dot_general(rows, table_of(second, h), NT, preferred_element_type=jnp.float32)
        mapped = ((a + scale[0:1, :]) * (b + scale[1:2, :])) * scale[3:4, :]
        maps.append(mapped.astype(jnp.bfloat16))
    positions = lax.broadcasted_iota(jnp.int32, (count, 1), 0) + info[0] * count
    begin = request_of(jnp.zeros((1, 1), jnp.int32) + info[0] * count, lengths)
    follows = jnp.where(request_of(positions, lengths) == begin, 1.0, 0.0)
    for h in range(heads):
        cross = jnp.dot(maps[h], carried[h], preferred_element_type=jnp.float32)
        cols = slice(h * width, (h + 1) * width)
        combined = within[:, cols].astype(jnp.float32) + follows * cross
        factor = lax.rsqrt(jnp.mean(combined * combined, axis=-1, keepdims=True) + EPSILON)
        normed[:, cols] = (combined * factor * gains[:, cols]).astype(jnp.bfloat16)


def out_block(layout, tile, blocks, info, normed, pieces, near):
    depth = normed.shape[1]
    step = depth // 4
    pair = (near, near + blocks // 2)
    total = None
    for row in range(0, depth, step):
        both = jnp.concatenate(
            [piece_rows(pieces, layout, slot, row, step) for slot in pair], axis=1
        )
        term = jnp.dot(normed[:, row : row + step], both, preferred_element_type=jnp.float32)
        total = term if total is None else total + term
    found = []
    for k, slot in enumerate(pair):
        place = place_of(info[0], slot)
        at = jnp.where(place // (blocks // 2) == info[1], 0, blocks // 2) + place % (blocks // 2)
        found.append((at, total[:, k * tile : (k + 1) * tile].astype(jnp.bfloat16)))
    return found


def out_kernel(layout, tile, blocks, info, normed, *refs):
    pieces, (out,) = refs[: len(layout)], refs[len(layout) :]
    for near in range(blocks // 2):
        if near != blocks // 4:
            for at, part in out_block(layout, tile, blocks, info, normed, pieces, near):
                out[at] = part


def last_kernel(layout, tile, blocks, info, normed, *refs):
    pieces, (_, out, held, done) = refs[: len(layout)], refs[len(layout) :]
    copies = []
    for at, part in out_block(layout, tile, blocks, info, normed, pieces, blocks // 4):
        k = len(copies)
        held[k] = part
        copies.append(pltpu.make_async_copy(held.at[k], out.at[at], done.at[k]))
        copies[-1].start()
    for copy in copies:
        copy.wait()


def add_kernel(partial, received, out):
    tile = partial.shape[2]
    for k in range(received.shape[0]):
        total = partial[k].astype(jnp.float32) + received[k].astype(jnp.float32)
        out[:, k * tile : (k + 1) * tile] = total.astype(jnp.bfloat16)


def stay(array):
    return pltpu.with_memory_space_constraint(array, pltpu.HBM)


def call(kernel, name, mebibytes, cost, shapes, scalars, arrays, late=(), far=(), out_far=(), flush=False):
    shapes = [jax.ShapeDtypeStruct(shape, kind) for shape, kind in shapes]
    n, m, k = len(scalars), len(arrays), len(shapes)
    held = [arrays[i] for i in far] + [shapes[i] for i in out_far]
    arrays = [stay(array) if i in far else array for i, array in enumerate(arrays)]
    shapes = [
        pltpu.HBM(shape.shape, shape.dtype) if i in out_far else shape
        for i, shape in enumerate(shapes)
    ]
    scratch = [pltpu.VMEM(array.shape, array.dtype) for array in held]
    if held:
        scratch.append(pltpu.SemaphoreType.DMA((len(held),)))

    def body(*refs):
        given, made = list(refs[: n + m]), list(refs[n + m + len(late) :])
        outs, buffers = made[:k], made[k:]
        copies = []
        for at, i in enumerate(far):
            copies.append(pltpu.make_async_copy(given[n + i], buffers[at], buffers[-1].at[at]))
            given[n + i] = buffers[at]
        for copy in copies:
            copy.start()
        for copy in copies:
            copy.wait()
        copies = []
        for at, i in enumerate(out_far, len(far)):
            copies.append(pltpu.make_async_copy(buffers[at], outs[i], buffers[-1].at[at]))
            outs[i] = buffers[at]
        if flush:
            kernel(*given, *outs, flush=[copy.start for copy in copies])
        else:
            kernel(*given, *outs)
            for copy in copies:
                copy.start()
        for copy in copies:
            copy.wait()

    return pl.pallas_call(
        body,
        out_shape=shapes,
        in_specs=[SMEM] * n
        + [HBM if i in far else VMEM for i in range(m)]
        + [ANY] * len(late),
        out_specs=[HBM if i in out_far else VMEM for i in range(k)],
        scratch_shapes=scratch,
        compiler_params=params(mebibytes),
        cost_estimate=pl.CostEstimate(flops=cost[0], bytes_accessed=cost[1], transcendentals=0),
        name=name,
    )(*scalars, *arrays, *late)


def per_device_fast(
    tokens,
    q_weight,
    k_weight,
    v_weight,
    adapter_down,
    adapter_up,
    lengths,
    adapter_ids,
    head_gain,
    out_weight,
):
    count, depth = tokens.shape
    blocks = lax.axis_size("dp")
    heads = q_weight.shape[1] // F
    width = v_weight.shape[1] // heads
    rows = v_weight.shape[0]
    wide, small, total = heads * width, heads * F, heads * (width + 2 * F)
    tile = out_weight.shape[1]
    half = jnp.bfloat16
    info = jnp.stack([lax.axis_index("dp"), lax.axis_index("mp")]).astype(jnp.int32)
    first, second, scale = feature_tables()

    alone, pair = join(v_weight, q_weight, k_weight)
    other = lax.ppermute(adapter_down, "mp", [(0, 1), (1, 0)])
    (turned,) = call(
        functools.partial(turn_kernel, rows), "turn", 8, (0, 4 * count * depth),
        [((count, depth), half)], [info], [tokens],
    )
    (low,) = call(
        low_kernel, "low", 8, (4 * count * depth * adapter_down.shape[1], 2 * count * depth),
        [((count, 2 * adapter_down.shape[1]), half)], [info, lengths, adapter_ids],
        [tokens, adapter_down, other],
    )

    chain = gather_rows(alone, pair)
    next(chain)
    second_round = chain.send(())
    third = next(chain)
    out_alone, out_pair = pack(
        [[(0, 0, wide // 2)], [(0, wide // 2, wide // 2)]], [out_weight], second_round[:2] + (turned, low)
    )
    out_chain = gather_rows(out_alone, out_pair)
    out_first = next(out_chain)
    chain.send(out_first)
    out_second = out_chain.send(third[:2])
    fifth = chain.send(())
    gathered = next(chain)
    out_third = next(out_chain)

    pieces, layout = [piece for piece, _ in gathered], [places for _, places in gathered]
    query, keys, values, state = call(
        functools.partial(project_kernel, layout, rows, heads, width), "project", 14,
        (count * depth * total // 2, depth * total // 2),
        [
            ((count, small), half),
            ((count, small), half),
            ((count, wide), half),
            ((heads, FEATS, width), half),
        ],
        [info, lengths], [turned, low, adapter_up, first, second, scale.T, *pieces], out_far=(0, 1, 2), flush=True,
    )
    parts = state.reshape(blocks, heads * FEATS // blocks, width)
    parts = lax.all_to_all(parts, "dp", 0, 0, tiled=True)
    (within,) = call(
        functools.partial(within_kernel, heads, width), "within", 12,
        (12 * count * count * wide, 24 * count * wide), [((count, wide), half)],
        [info, lengths], [query, keys, values], far=(0, 1, 2),
    )
    out_fourth = out_chain.send(())
    (mixed,) = call(
        functools.partial(mix_kernel, blocks, count), "mix", 4, (0, 4 * parts.size),
        [(parts.shape, half)], [lengths], [parts], (within,),
    )
    carried = lax.all_to_all(mixed, "dp", 0, 0, tiled=True).reshape(heads, FEATS, width)
    (normed,) = call(
        functools.partial(finish_kernel, heads, width), "finish", 10,
        (2 * count * FEATS * wide, 8 * count * wide), [((count, wide), half)],
        [info, lengths],
        [within, query, carried, head_gain.reshape(1, -1), first, second, scale], far=(1, 4, 5, 6),
    )
    out_chain.send((normed,))
    out_gathered = next(out_chain)
    far_slots = (blocks // 4, 3 * blocks // 4)
    early = [(p, l) for p, l in out_gathered if not all(place[0] in far_slots for place in l)]
    last = [(p, l) for p, l in out_gathered if any(place[0] in far_slots for place in l)]
    (partial,) = call(
        functools.partial(out_kernel, [l for _, l in early], tile, blocks), "out", 12,
        (2 * count * wide * blocks * tile, 4 * count * blocks * tile),
        [((blocks, count, tile), half)], [info], [normed] + [p for p, _ in early],
    )
    partial = pl.pallas_call(
        functools.partial(last_kernel, [l for _, l in last], tile, blocks),
        out_shape=jax.ShapeDtypeStruct(partial.shape, partial.dtype),
        in_specs=[SMEM] + [VMEM] * (1 + len(last)) + [ANY],
        out_specs=ANY,
        scratch_shapes=[
            pltpu.VMEM((2, count, tile), half),
            pltpu.SemaphoreType.DMA((2,)),
        ],
        input_output_aliases={2 + len(last): 0},
        compiler_params=params(8),
        name="last",
    )(info, normed, *[p for p, _ in last], partial)
    received = lax.ppermute(partial[blocks // 2 :], "mp", [(0, 1), (1, 0)])
    (result,) = call(
        add_kernel, "add", 8, (0, 8 * count * wide), [((count, blocks // 2 * tile), half)], [],
        [partial, received],
    )
    return result


def solution(mesh):
    placed = (
        P("dp", None),
        P("dp", "mp"),
        P("dp", "mp"),
        P("dp", "mp"),
        P(None, "mp"),
        P(None, "mp"),
        P(),
        P(),
        P("mp"),
        P("mp", "dp"),
    )
    fast = mesh.shape["dp"] == 16 and mesh.shape["mp"] == 2
    return jax.shard_map(
        per_device_fast if fast else per_device_general,
        mesh=mesh,
        in_specs=placed,
        out_specs=P("dp", "mp"),
        check_vma=False,
    )
```
